256 devices in a mesh: blk: 64 (over y, z, x_lo), sub: 4 (over x_hi, core).
Axes of the slice: x: 4 (x_hi: 2, x_lo: 2; x = x_hi * 2 + x_lo), y: 4, z: 8, core: 2. Of those that a mesh axis runs over, the one named last changes fastest.
Arguments:
- vorticity: float32 [512, 3, 32768], P(('blk', 'sub')), may hold values from -4.5 to 4.5
- velocity: float32 [512, 3, 32768], P(('blk', 'sub')), may hold values from -6 to 6
- level_map: int32 [512], P(('blk', 'sub')), may hold values from 0 to 2
- patch_owner: int32 [512], P(('blk', 'sub')), may hold values from 0 to 255
- neighbours: int32 [512, 6], P(('blk', 'sub')), may hold values from 0 to 23
- fish_slot: int32 [256], P(('blk', 'sub')), may hold values from 0 to 1, as said below
- fish_mask: float32 [256, 32768], P(('blk', 'sub')), may hold values from 0 to 1
- fish_speed: float32 [256, 3], P(('blk', 'sub')), may hold values from -4 to 4
Outputs:
- vorticity_next: float32 [512, 3, 32768], P(('blk', 'sub'))
- velocity_next: float32 [512, 3, 32768], P(('blk', 'sub'))
The draws below stay inside these ranges and needn't reach their ends.
Inputs may be any that keep to these rules, and one draw needn't show every extreme that they name: `fish_slot`: the 1 entries of one device name distinct slots of that device's 2 blocks.
All inputs are finite; a program needn't handle non-finite values.
Results may differ from the reference program's by a relative error of at most 0.000086.
Values sent between devices are 32-bit elements; how exact they have to be, the bound alone decides.
A program may use at most 192 MiB of HBM per device.

```python
import math
import jax
import jax.numpy as jnp
import numpy as np
from jax import lax

EDGE = 32
NB_SUB = 2
FISH_DEV = 1
GX = 32
GY = 128
GZ = 4
CELLS = 32768
GROUP = 8
NBLK = 512
NFISH = 256
PATCHES = 256


def draw_fish_slot(key, part):
    key = jax.random.fold_in(key, 11)
    devices = NFISH // FISH_DEV
    keys = jax.random.split(key, devices)
    picks = jax.vmap(lambda single: jax.random.permutation(single, NB_SUB)[:FISH_DEV])(keys)
    return picks.reshape(NFISH).astype(jnp.int32)


def draw_vorticity(key, part):
    key = jax.random.fold_in(key, 5)
    noise_key, size_key, sign_key = jax.random.split(key, 3)
    noise = jax.random.truncated_normal(noise_key, -3.0, 3.0, (NBLK, 3, CELLS), jnp.float32)
    size = jax.random.uniform(size_key, (NBLK, 3, 1), jnp.float32, 0.5, 1.5)
    sign = jnp.where(jax.random.bernoulli(sign_key, 0.5, (NBLK, 3, 1)), 1.0, -1.0)
    return (noise + sign * size).astype(jnp.float32)


def set_ends(values, own_key, least, largest):
    dims = values.shape
    spot = [jax.random.randint(jax.random.fold_in(own_key, axis), (), 0, dims[axis]) for axis in range(len(dims))]
    values = values.at[tuple(spot)].set(least)
    longest = dims.index(max(dims))
    spot[longest] = (spot[longest] + 1) % dims[longest]
    return values.at[tuple(spot)].set(largest)


def steps_of(rng, shape, cuts, smallest, high):
    def one(dim, blocks):
        draws = jax.random.uniform(jax.random.fold_in(jax.random.fold_in(rng, 6), dim), (blocks,), jnp.float32, smallest / len(cuts), high / len(cuts))
        return jnp.repeat(jnp.exp(draws), shape[dim] // blocks).reshape((-1,) + (1,) * (len(shape) - dim - 1))

    gain = one(*cuts[0])
    for cut in cuts[1:]:
        gain = gain * one(*cut)
    return gain


def cumulative_ranks(amount, lean):
    loads = [(1 << 20) // math.isqrt(rank ** lean) + 1 for rank in range(1, amount + 1)]
    spread = 1 + sum(loads) // (1 << 30)
    return np.cumsum(np.array([max(1, weight // spread) for weight in loads]))


def skewed_ids(key, dims, count, lean):
    table = cumulative_ranks(count, lean)
    lot = jax.random.randint(jax.random.fold_in(key, 1), dims, 0, int(table[count - 1]))
    grade = jnp.searchsorted(jnp.asarray(table, jnp.int32), lot, side="right")
    return jax.random.permutation(jax.random.fold_in(key, 2), count)[grade].astype(jnp.int32)


def gaussian(stream_key, extent, spread, reach, pieces=(), held_as=jnp.bfloat16):
    values = spread * jax.random.normal(stream_key, extent, jnp.float32)
    if pieces:
        values = values * steps_of(stream_key, extent, pieces, -0.22, 0.18)
    return jnp.clip(values, -reach, reach).astype(held_as)


def setup_inputs(seed: int = 0) -> dict:
    key_of = jax.random.split(jax.random.key(seed), 9)
    vorticity = draw_vorticity(jax.random.fold_in(key_of[8], 71), 0)
    velocity = gaussian(key_of[1], (NBLK, 3, CELLS), 1.0, 6.0, ((0, 256),), jnp.float32)
    level_map = set_ends(jax.random.randint(key_of[2], (NBLK,), 0, 3), jax.random.fold_in(key_of[2], 1), 0, 2).astype(jnp.int32)
    patch_owner = set_ends(skewed_ids(key_of[3], (NBLK,), PATCHES, 1), jax.random.fold_in(key_of[3], 3), 0, PATCHES - 1).astype(jnp.int32)
    neighbours = set_ends(jax.random.randint(key_of[4], (NBLK, 6), 0, 3 * GROUP), jax.random.fold_in(key_of[4], 1), 0, (3 * GROUP) - 1).astype(jnp.int32)
    fish_slot = draw_fish_slot(jax.random.fold_in(key_of[8], 71), 0)
    fish_mask = jnp.clip(1.0 * jax.random.uniform(key_of[6], (NFISH, CELLS), jnp.float32) ** steps_of(key_of[6], (NFISH, CELLS), ((0, 256),), -0.2, 0.2), 0.0, 1.0)
    fish_speed = gaussian(key_of[7], (NFISH, 3), 1.0, 4.0, ((0, 256),), jnp.float32)
    return {"vorticity": vorticity, "velocity": velocity, "level_map": level_map, "patch_owner": patch_owner, "neighbours": neighbours, "fish_slot": fish_slot, "fish_mask": fish_mask, "fish_speed": fish_speed}


TIME_STEP = 0.05
VISCOSITY = 0.1
PENALTY = 10.0


def face_planes(field):
    width = field.shape[0]
    edge = field.shape[1]
    planes = [field[:, 0], field[:, -1], field[:, :, 0], field[:, :, -1], field[:, :, :, 0], field[:, :, :, -1]]
    return jnp.stack([plane.reshape(width, edge * edge) for plane in planes])


def with_ghosts(field, ghosts):
    width = field.shape[0]
    edge = field.shape[1]
    sheet = ghosts.reshape(6, width, edge, edge)
    padded = jnp.pad(field, ((0, 0), (1, 1), (1, 1), (1, 1)))
    padded = padded.at[:, 0, 1:-1, 1:-1].set(sheet[0])
    padded = padded.at[:, -1, 1:-1, 1:-1].set(sheet[1])
    padded = padded.at[:, 1:-1, 0, 1:-1].set(sheet[2])
    padded = padded.at[:, 1:-1, -1, 1:-1].set(sheet[3])
    padded = padded.at[:, 1:-1, 1:-1, 0].set(sheet[4])
    padded = padded.at[:, 1:-1, 1:-1, -1].set(sheet[5])
    return padded


def advance(field, ghosts, level):
    padded = with_ghosts(field, ghosts)
    spacing = jnp.power(0.5, level.astype(jnp.float32))
    centre = padded[:, 1:-1, 1:-1, 1:-1]
    lower = [padded[:, :-2, 1:-1, 1:-1], padded[:, 1:-1, :-2, 1:-1], padded[:, 1:-1, 1:-1, :-2]]
    upper = [padded[:, 2:, 1:-1, 1:-1], padded[:, 1:-1, 2:, 1:-1], padded[:, 1:-1, 1:-1, 2:]]
    slopes = [(upper[which] - lower[which]) / (2.0 * spacing) for which in range(3)]
    vort = centre[:3]
    veloc = centre[3:]
    stretch = vort[0] * slopes[0][3:] + vort[1] * slopes[1][3:] + vort[2] * slopes[2][3:]
    carried = veloc[0] * slopes[0][:3] + veloc[1] * slopes[1][:3] + veloc[2] * slopes[2][:3]
    beside_all = upper[0][:3] + lower[0][:3] + upper[1][:3] + lower[1][:3] + upper[2][:3] + lower[2][:3]
    laplace = (beside_all - 6.0 * vort) / (spacing * spacing)
    return vort + TIME_STEP * (stretch - carried + VISCOSITY * laplace)


def restrict(vort, level):
    edge = vort.shape[1]
    ratio = edge // 4
    cubes = vort.reshape(3, 4, ratio, 4, ratio, 4, ratio)
    return jnp.mean(cubes, axis=(2, 4, 6)) * jnp.power(0.125, level.astype(jnp.float32))


def to_grid(columns):
    parts = columns.reshape(3, 4, 4, 4, GX // 4, GY // 4, GZ // 4)
    return parts.transpose(0, 6, 3, 4, 1, 5, 2).reshape(3, GZ, GX, GY)


def from_grid(grid):
    parts = grid.reshape(3, GZ // 4, 4, GX // 4, 4, GY // 4, 4)
    return parts.transpose(0, 4, 6, 2, 3, 5, 1).reshape(3, 4, 4, 4, PATCHES)


def waves(count, length, first):
    index = jnp.arange(count, dtype=jnp.int32) + first
    signed = jnp.where(index < (length + 1) // 2, index, index - length).astype(jnp.float32)
    full = signed * (2.0 * math.pi / length)
    slope = jnp.where(index == length // 2, 0.0, full)
    return full, slope


def biot_savart(real_part, imag_part, yfirst):
    count_z, count_x, count_y = real_part.shape[1:]
    full_z, slope_z = waves(count_z, GZ, 0)
    full_x, slope_x = waves(count_x, GX, 0)
    full_y, slope_y = waves(count_y, GY, yfirst)
    square = full_z[:, None, None] ** 2 + full_x[None, :, None] ** 2 + full_y[None, None, :] ** 2
    inverse_sq = jnp.where(square > 0, 1.0 / jnp.where(square > 0, square, 1.0), 0.0)
    slope_z = slope_z[:, None, None]
    slope_x = slope_x[None, :, None]
    slope_y = slope_y[None, None, :]

    def cross(spectrum):
        psi_x = spectrum[0] * inverse_sq
        psi_y = spectrum[1] * inverse_sq
        psi_z = spectrum[2] * inverse_sq
        return jnp.stack([slope_y * psi_z - slope_z * psi_y, slope_z * psi_x - slope_x * psi_z, slope_x * psi_y - slope_y * psi_x])

    cross_real = cross(real_part)
    cross_imag = cross(imag_part)
    return -cross_imag, cross_real


def upsample(patch, ratio):
    large = jnp.broadcast_to(patch[:, :, None, :, None, :, None], (3, 4, ratio, 4, ratio, 4, ratio))
    return large.reshape(3, 64 * ratio ** 3)


def reference(vorticity, velocity, level_map, patch_owner, neighbours, fish_slot, fish_mask, fish_speed):
    total = vorticity.shape[0]
    fields = jnp.concatenate([vorticity, velocity], axis=1).reshape(total, 6, EDGE, EDGE, EDGE)
    faces = lax.map(face_planes, fields)
    blocks = jnp.arange(total, dtype=jnp.int32)
    source = ((blocks // GROUP) - 1)[:, None] * GROUP + neighbours
    valid = (source >= 0) & (source < total)
    opposite = jnp.bitwise_xor(jnp.arange(6, dtype=jnp.int32), 1)
    flat = (jnp.where(valid, source, 0) * 6 + opposite[None, :]).astype(jnp.int32)
    table = faces.reshape(total * 6, 6, EDGE * EDGE)
    ghosts = jnp.where(valid[:, :, None, None], table[flat], 0.0)
    fresh = lax.map(lambda item: advance(item[0], item[1], item[2]), (fields, ghosts, level_map))
    restricted = jax.vmap(restrict)(fresh, level_map)
    columns = jax.ops.segment_sum(restricted.reshape(total, 192), patch_owner, num_segments=PATCHES)
    source_grid = to_grid(columns.T)
    spectrum = jnp.fft.fftn(source_grid, axes=(1, 2, 3))
    speed_real, speed_imag = biot_savart(jnp.real(spectrum), jnp.imag(spectrum), 0)
    coarse_velocity = jnp.real(jnp.fft.ifftn(lax.complex(speed_real, speed_imag), axes=(1, 2, 3)))
    patches = jnp.take(from_grid(coarse_velocity), patch_owner, axis=4)
    ratio = EDGE // 4
    lifted = jax.vmap(lambda patch: upsample(patch, ratio))(patches.transpose(4, 0, 1, 2, 3))
    blended = velocity + lifted
    entries = jnp.arange(fish_slot.shape[0], dtype=jnp.int32)
    owners = ((entries // FISH_DEV) * NB_SUB + fish_slot).astype(jnp.int32)
    chi = jnp.zeros((total, CELLS), jnp.float32).at[owners].set(fish_mask)
    speed = jnp.zeros((total, 3), jnp.float32).at[owners].set(fish_speed)
    velocity_next = (blended + PENALTY * chi[:, None, :] * speed[:, :, None]) / (1.0 + PENALTY * chi[:, None, :])
    return fresh.reshape(total, 3, CELLS), velocity_next
```

```python
import functools
import math

import jax
import jax.numpy as jnp
import numpy as np
from jax import lax
from jax.experimental import pallas as pl
from jax.experimental.pallas import tpu as pltpu
from jax.sharding import PartitionSpec as P

MESH = pl.DeviceIdType.MESH
HIGHEST = lax.Precision.HIGHEST
RINGS = 32
GX = 32
GY = 128
GZ = 4


def dft_tables():
    space = np.arange(128)
    px, ix, iz = space // 16, (space // 4) % 4, space % 4
    x, z = 4 * px + ix, iz
    kx, kz = space // 4, space % 4
    iy, py = space // 32, space % 32
    y = 4 * py + iy
    ky = space
    theta = 2.0 * np.pi * ((kx[:, None] * x[None, :] % 32) / 32.0 + (kz[:, None] * z[None, :] % 4) / 4.0)
    phi = 2.0 * np.pi * ((y[:, None] * ky[None, :]) % 128) / 128.0
    fwd_y = np.concatenate([np.cos(phi), -np.sin(phi)], axis=1)
    fwd_xz = np.concatenate([np.cos(theta), np.sin(theta)], axis=0)
    inv_xz = np.concatenate([np.cos(theta.T), np.sin(theta.T)], axis=0)
    inv_y = np.concatenate([np.cos(phi.T), -np.sin(phi.T)], axis=0) / 16384.0

    def waves(index, length):
        signed = np.where(index < (length + 1) // 2, index, index - length)
        full = signed * (2.0 * math.pi / length)
        return full, np.where(index == length // 2, 0.0, full)

    full_x, slope_x = waves(kx, GX)
    full_y, slope_y = waves(ky, GY)
    full_z, slope_z = waves(kz, GZ)
    square = (full_x**2 + full_z**2)[:, None] + (full_y**2)[None, :]
    inverse = np.where(square > 0, 1.0 / np.where(square > 0, square, 1.0), 0.0)
    one = np.ones((128, 128))
    spectral = np.concatenate([inverse, slope_x[:, None] * one, slope_y[None, :] * one, slope_z[:, None] * one])
    return tuple(a.astype(np.float32) for a in (fwd_y, fwd_xz, inv_xz, inv_y, spectral))


def fold_tables():
    row = np.arange(192)
    lane = np.arange(128)
    n = np.arange(256)
    row_c_ix, row_iy, row_b = row // 16, (row % 16) // 4, row % 2
    lane_iz = (lane % 32) // 8
    live = n < 192
    fold = ((lane_iz[:, None] == n[None, :] % 4) & live[None, :]) * 1.0
    pick = ((n[None, :] // 4 == (row_iy * 12 + row_c_ix)[:, None]) & live[None, :]) * 1.0
    mean = (np.arange(8)[:, None] == row_b[None, :]) / 512.0
    src = np.arange(96)
    src_c, src_b, src_ix, src_iz = src // 32, (src // 16) % 2, (src // 4) % 4, src % 4
    spread_y = (lane[None, :] // 32 == row_iy[:, None]) * 1.0
    match = ((src_c * 4 + src_ix)[None, :] == row_c_ix[:, None]) & (src_b[None, :] == row_b[:, None])
    spread_z = (src_iz[:, None] == lane_iz[None, :]) * 1.0
    return tuple(a.astype(np.float32) for a in (fold, pick, mean, spread_y, match * 1.0, spread_z))


def iota(shape, dim):
    return lax.broadcasted_iota(jnp.int32, shape, dim)


def place():
    blk, sub = lax.axis_index("blk"), lax.axis_index("sub")
    return blk // 2, lax.rem(blk, 2), sub


def faces_kernel(nb_ref, w_ref, u_ref, out_ref, s1, r1, s2, r2, tmp, nbs, nbr, ssem, rsem):
    ring, half, sub = place()
    me = half * 4 + sub

    def mate(k):
        other = lax.bitwise_xor(me, k)
        return (ring * 2 + other // 4, lax.rem(other, 4))

    def beside(step):
        return (lax.rem(ring + step + RINGS, RINGS) * 2 + half, sub)

    barrier = pltpu.get_barrier_semaphore()
    for k in range(1, 8):
        pl.semaphore_signal(barrier, inc=1, device_id=mate(k), device_id_type=MESH)
    for step in (-1, 1):
        pl.semaphore_signal(barrier, inc=1, device_id=beside(step), device_id_type=MESH)

    lane = iota((8, 128), 1)
    row = iota((8, 128), 0)
    wants = jnp.zeros((8, 128), jnp.int32)
    for b in range(2):
        for f in range(6):
            wants = jnp.where(lane == b * 6 + f, nb_ref[b, f] + half * 8, wants)
    nbs[...] = wants
    nbr[pl.ds(pl.multiple_of(me * 8, 8), 8), :] = wants

    def source(c):
        return (w_ref, u_ref)[c // 3], (c % 3) * 512

    def put(b, f, c, plane):
        s1[pl.ds((b * 6 + f) * 6 + c, 8, stride=72), :] = plane

    for c in range(6):
        ref, base = source(c)
        for b in range(2):
            for f, x in ((0, 0), (1, 31)):
                put(b, f, c, ref[pl.ds(base + x * 16 + b, 8, stride=2), :])
            low = high = jnp.zeros((8, 128), jnp.float32)
            for g in range(4):
                first = ref[pl.ds(base + g * 128 + b, 8, stride=16), :]
                last = ref[pl.ds(base + g * 128 + 14 + b, 8, stride=16), :]
                if g:
                    first = pltpu.roll(first, 32 * g, 1)
                if g != 3:
                    last = pltpu.roll(last, (32 * g + 32) % 128, 1)
                here = lane // 32 == g
                low = jnp.where(here, first, low)
                high = jnp.where(here, last, high)
            put(b, 2, c, low)
            put(b, 3, c, high)

    def gather_z(x, held):
        at_low = (lane & 31) == x
        at_high = (lane & 31) == ((x + 31) & 31)
        fresh = []
        for c in range(6):
            ref, base = source(c)
            for h in range(2):
                plane = ref[pl.ds(pl.multiple_of(base + x * 16 + h * 8, 8), 8), :]
                turned = pltpu.roll(plane, x, 1)
                low, high = held[(c * 2 + h) * 2], held[(c * 2 + h) * 2 + 1]
                fresh += [jnp.where(at_low, turned, low), jnp.where(at_high, turned, high)]
        return tuple(fresh)

    zero = jnp.zeros((8, 128), jnp.float32)
    packed = lax.fori_loop(0, 32, gather_z, (zero,) * 24)
    for c in range(6):
        for which in range(2):
            for h in range(2):
                at = (c * 2 + which) * 16 + h * 8
                tmp[at : at + 8, :] = packed[(c * 2 + h) * 2 + which]
    for c in range(6):
        for which in range(2):
            for b in range(2):
                put(b, 4 + which, c, tmp[pl.ds((c * 2 + which) * 16 + b, 8, stride=2), :])

    pl.semaphore_wait(barrier, 9)
    copies = []
    for k in range(1, 8):
        at = pl.ds(pl.multiple_of(me * 8, 8), 8)
        copies.append(pltpu.make_async_remote_copy(
            src_ref=nbs, dst_ref=nbr.at[at], send_sem=ssem.at[k], recv_sem=rsem.at[k],
            device_id=mate(k), device_id_type=MESH))
        other = lax.bitwise_xor(me, k)
        copies.append(pltpu.make_async_remote_copy(
            src_ref=s1.at[pl.ds(pl.multiple_of(other * 72, 8), 72)],
            dst_ref=r1.at[pl.ds(pl.multiple_of((4 + me) * 72, 8), 72)],
            send_sem=ssem.at[8 + k], recv_sem=rsem.at[8 + k],
            device_id=mate(k), device_id_type=MESH))
    for copy in copies:
        copy.start()
    r1[pl.ds(pl.multiple_of((4 + me) * 72, 8), 72), :] = s1[pl.ds(pl.multiple_of(me * 72, 8), 72), :]
    for copy in copies:
        copy.wait()

    copies = []
    for which, (src, dst, step) in enumerate(((8, 0, 1), (4, 12, -1))):
        copies.append(pltpu.make_async_remote_copy(
            src_ref=r1.at[pl.ds(src * 72, 288)], dst_ref=r1.at[pl.ds(dst * 72, 288)],
            send_sem=ssem.at[16 + which], recv_sem=rsem.at[16 + which],
            device_id=beside(step), device_id_type=MESH))
    for copy in copies:
        copy.start()
    for copy in copies:
        copy.wait()

    wanted = nbr[pl.ds(0, 8, stride=8), :]
    dead_low = (ring == 0).astype(jnp.int32)
    dead_high = (ring == RINGS - 1).astype(jnp.int32)
    slot = iota((8, 32), 1)
    alive = 1 - dead_low * (slot < 8).astype(jnp.int32) - dead_high * (slot >= 24).astype(jnp.int32)
    alive = alive.astype(jnp.float32)
    for f in range(6):
        hot = jnp.concatenate(
            [jnp.where(wanted[:, b * 6 + f : b * 6 + f + 1] == slot, alive, 0.0) for b in range(2)], axis=0)
        data = jnp.concatenate(
            [r1[pl.ds((f ^ 1) * 6 + c, 32, stride=36), :] for c in range(6)], axis=1)
        got = jnp.dot(hot, data, precision=HIGHEST, preferred_element_type=jnp.float32)
        for b in range(2):
            for c in range(6):
                s2[pl.ds((b * 6 + f) * 6 + c, 8, stride=72), :] = got[b * 8 : b * 8 + 8, c * 128 : c * 128 + 128]

    copies = []
    for k in range(1, 8):
        other = lax.bitwise_xor(me, k)
        copies.append(pltpu.make_async_remote_copy(
            src_ref=s2.at[pl.ds(pl.multiple_of(other * 72, 8), 72)],
            dst_ref=r2.at[pl.ds(pl.multiple_of(me * 72, 8), 72)],
            send_sem=ssem.at[18 + k], recv_sem=rsem.at[18 + k],
            device_id=mate(k), device_id_type=MESH))
    for copy in copies:
        copy.start()
    r2[pl.ds(pl.multiple_of(me * 72, 8), 72), :] = s2[pl.ds(pl.multiple_of(me * 72, 8), 72), :]
    for copy in copies:
        copy.wait()
    out_ref[...] = r2[...]


def row_pair(first, second):
    return jnp.where((iota((8, 128), 0) & 1) == 0, first, second)


def stencil_kernel(level_ref, owner_ref, w_ref, u_ref, gh_ref, fold_ref, pick_ref, mean_ref,
                   out_ref, tile_ref, gx, gy, gz, acc):
    lane = iota((8, 128), 1)
    row = iota((8, 128), 0)

    def ghost(b, f, c):
        return gh_ref[pl.ds((b * 6 + f) * 6 + c, 8, stride=72), :]

    for c in range(6):
        for b in range(2):
            for f in range(2):
                gx[pl.ds((f * 6 + c) * 16 + b, 8, stride=2), :] = ghost(b, f, c)
                gz[pl.ds((f * 6 + c) * 16 + b, 8, stride=2), :] = ghost(b, 4 + f, c)
            low, high = ghost(b, 2, c), ghost(b, 3, c)
            for g in range(4):
                at = (c * 32 + g * 8) * 8 + b
                gy[pl.ds(at, 8, stride=8), :] = pltpu.roll(low, 96 - 32 * g, 1) if g != 3 else low
                gy[pl.ds(at + 6, 8, stride=8), :] = pltpu.roll(high, 128 - 32 * g, 1) if g else high
    acc[...] = jnp.zeros_like(acc)

    def scale(level):
        return lax.shift_left(1, level).astype(jnp.float32)

    size = row_pair(scale(level_ref[0]), scale(level_ref[1]))
    slope = (0.05 * 0.5) * size
    spread = (0.05 * 0.1) * (size * size)

    def around(x, c, h):
        ref = (w_ref, u_ref)[c // 3]
        at = (c % 3) * 32 + x
        rows = slice(h * 8, h * 8 + 8)
        here = ref[at, rows, :]
        if isinstance(x, int) and x == 0:
            left = gx[c * 16 + h * 8 : c * 16 + h * 8 + 8, :]
        else:
            left = ref[at - 1, rows, :]
        if isinstance(x, int) and x == 31:
            right = gx[(6 + c) * 16 + h * 8 : (6 + c) * 16 + h * 8 + 8, :]
        else:
            right = ref[at + 1, rows, :]
        side = gy[pl.ds(pl.multiple_of((c * 32 + x) * 8, 8), 8), :]
        if h == 0:
            before = jnp.where(row < 2, side, pltpu.roll(here, 2, 0))
            after = ref[at, 2:10, :]
        else:
            before = ref[at, 6:14, :]
            after = jnp.where(row >= 6, side, pltpu.roll(here, 6, 0))
        before = pltpu.roll(jnp.where(lane >= 96, before, here), 32, 1)
        after = pltpu.roll(jnp.where(lane < 32, after, here), 96, 1)
        below = gz[c * 16 + h * 8 : c * 16 + h * 8 + 8, :]
        above = gz[(6 + c) * 16 + h * 8 : (6 + c) * 16 + h * 8 + 8, :]
        below = jnp.where((lane & 31) == 0, pltpu.roll(below, (97 - x) & 127, 1), pltpu.roll(here, 1, 1))
        above = jnp.where((lane & 31) == 31, pltpu.roll(above, (31 - x) & 127, 1), pltpu.roll(here, 127, 1))
        return here, (left, right), (before, after), (below, above)

    def plane(x):
        for h in range(2):
            parts = [around(x, c, h) for c in range(6)]
            heres = [part[0] for part in parts]
            slopes = [[part[1 + d][1] - part[1 + d][0] for d in range(3)] for part in parts]
            for i in range(3):
                turn = heres[0] * slopes[3 + i][0] + heres[1] * slopes[3 + i][1] + heres[2] * slopes[3 + i][2]
                turn -= heres[3] * slopes[i][0] + heres[4] * slopes[i][1] + heres[5] * slopes[i][2]
                ends = [part for d in range(3) for part in parts[i][1 + d]]
                total = (ends[0] + ends[1]) + (ends[2] + ends[3]) + (ends[4] + ends[5])
                fresh = heres[i] + slope * turn + spread * (total - 6.0 * heres[i])
                out_ref[i * 32 + x, h * 8 : h * 8 + 8, :] = fresh
                at = pl.multiple_of((i * 4 + x // 8) * 16 + h * 8, 8)
                acc[pl.ds(at, 8), :] += fresh

    plane(0)

    def step(x, carry):
        plane(x)
        return carry

    lax.fori_loop(1, 31, step, 0)
    plane(31)

    folded = jnp.dot(acc[...], fold_ref[...], precision=HIGHEST, preferred_element_type=jnp.float32)
    folded = folded * pick_ref[...]
    rows = jnp.dot(mean_ref[...], folded, precision=HIGHEST, preferred_element_type=jnp.float32)
    wide_row, wide_lane = iota((8, 256), 0), iota((8, 256), 1)

    def shrink(level):
        return jnp.where(level == 0, 1.0, jnp.where(level == 1, 0.125, 0.015625))

    rows = rows * jnp.where(wide_row == 0, shrink(level_ref[0]), shrink(level_ref[1]))
    owners = jnp.where(wide_row == 0, owner_ref[0], owner_ref[1]).astype(jnp.float32)
    rows = jnp.where(wide_lane == 192, owners, rows)
    tile_ref[...] = jnp.concatenate(
        [rows[0:1, 0:128], rows[0:1, 128:256], rows[1:2, 0:128], rows[1:2, 128:256], jnp.zeros((4, 128), jnp.float32)],
        axis=0)


def gather_kernel(tile_ref, out_ref, t1, g, ssem, rsem):
    ring, half, sub = place()
    me = half * 4 + sub
    y, z = ring // 8, lax.rem(ring, 8)

    def mate(k):
        other = lax.bitwise_xor(me, k)
        return (ring * 2 + other // 4, lax.rem(other, 4))

    def along_z(k):
        return ((y * 8 + lax.rem(z + k, 8)) * 2 + half, sub)

    def along_y(k):
        return ((lax.rem(y + k, 4) * 8 + z) * 2 + half, sub)

    everyone = [mate(k) for k in range(1, 8)] + [along_z(k) for k in range(1, 8)] + [along_y(k) for k in range(1, 4)]
    barrier = pltpu.get_barrier_semaphore()
    for device in everyone:
        pl.semaphore_signal(barrier, inc=1, device_id=device, device_id_type=MESH)
    pl.semaphore_wait(barrier, len(everyone))

    def spread(ref, targets, first):
        copies = [
            pltpu.make_async_remote_copy(
                src_ref=ref, dst_ref=ref, send_sem=ssem.at[first + n], recv_sem=rsem.at[first + n],
                device_id=device, device_id_type=MESH)
            for n, device in enumerate(targets)
        ]
        for copy in copies:
            copy.start()
        for copy in copies:
            copy.wait()

    mine = pl.ds(pl.multiple_of(me * 8, 8), 8)
    t1[mine, :] = tile_ref[...]
    spread(t1.at[mine], everyone[:7], 0)
    at = pl.ds(pl.multiple_of(ring * 8, 8), 8)
    for t in range(4):
        g[at, t * 128 : t * 128 + 128] = t1[pl.ds(t, 8, stride=8), :]
    spread(g.at[at], everyone[7:14], 7)
    spread(g.at[pl.ds(pl.multiple_of(y * 64, 64), 64)], everyone[14:], 14)
    out_ref[...] = g[...]


def solve_kernel(owner_ref, slot_ref, speed_ref, mask_ref, u_ref, g_ref, fwd_y, fwd_xz, inv_xz, inv_y, spectral,
                 spread_y, match, spread_z, out_ref, chi, field):
    dot = functools.partial(jnp.dot, precision=HIGHEST, preferred_element_type=jnp.float32)
    sent = jnp.concatenate([g_ref[:, 0:256], g_ref[:, 256:512]], axis=0)
    hot = (sent[:, 192:193] == iota((512, 256), 1).astype(jnp.float32)).astype(jnp.float32)
    columns = lax.dot_general(sent, hot, (((0,), (0,)), ((), ())), precision=HIGHEST, preferred_element_type=jnp.float32)
    lane = iota((48, 128), 1)
    rows = []
    for px in range(8):
        held = jnp.zeros((48, 128), jnp.float32)
        for iy in range(4):
            part = columns[iy * 48 : iy * 48 + 48, (px // 4) * 128 : (px // 4) * 128 + 128]
            turn = ((iy - px % 4) * 32) % 128
            if turn:
                part = pltpu.roll(part, turn, 1)
            held = jnp.where(lane // 32 == iy, part, held)
        rows.append(held)
    waves_y = dot(jnp.concatenate(rows, axis=0), fwd_y[...])
    stacked = jnp.concatenate(
        [
            jnp.concatenate([waves_y[px * 48 + c * 16 : px * 48 + c * 16 + 16, :] for px in range(8)], axis=0)
            for c in range(3)
        ],
        axis=1,
    )
    full = dot(fwd_xz[...], stacked)
    inverse, slope_x = spectral[0:128, :], spectral[128:256, :]
    slope_y, slope_z = spectral[256:384, :], spectral[384:512, :]
    psi_real, psi_imag = [], []
    for c in range(3):
        low = full[:, c * 256 : c * 256 + 128]
        high = full[:, c * 256 + 128 : c * 256 + 256]
        psi_real.append((low[0:128] + high[128:256]) * inverse)
        psi_imag.append((high[0:128] - low[128:256]) * inverse)

    def cross(psi):
        return [
            slope_y * psi[2] - slope_z * psi[1],
            slope_z * psi[0] - slope_x * psi[2],
            slope_x * psi[1] - slope_y * psi[0],
        ]

    cross_real, cross_imag = cross(psi_real), cross(psi_imag)
    hats = jnp.concatenate([part for c in range(3) for part in (-cross_imag[c], cross_real[c])], axis=1)
    owners = (owner_ref[0], owner_ref[1])
    chosen = jnp.concatenate(
        [
            inv_xz[pl.ds(pl.multiple_of(side * 128 + (owner // 32) * 16, 16), 16), :]
            for side in range(2)
            for owner in owners
        ],
        axis=0,
    )
    near = dot(chosen, hats)
    lines = []
    for c in range(3):
        low = near[:, c * 256 : c * 256 + 128]
        high = near[:, c * 256 + 128 : c * 256 + 256]
        lines.append(jnp.concatenate([low[0:32] - high[32:64], high[0:32] + low[32:64]], axis=1))
    patches = dot(jnp.concatenate(lines, axis=0), inv_y[...])
    row96, lane96 = iota((96, 128), 0), iota((96, 128), 1)
    column = jnp.where((row96 // 16) % 2 == 0, owners[0] % 32, owners[1] % 32)
    patches = jnp.where(lane96 % 32 == column, patches, 0.0)
    turned = lax.dot_general(spread_y[...], patches, (((1,), (1,)), ((), ())), precision=HIGHEST,
                             preferred_element_type=jnp.float32)
    field[...] = dot(turned * match[...], spread_z[...])

    slot = slot_ref[0]
    on = [jnp.where(slot == b, 10.0, 0.0) for b in range(2)]

    def plane(x, carry):
        solid = mask_ref[pl.ds(pl.multiple_of(x * 8, 8), 8), :]
        for b in range(2):
            chi[pl.ds(x * 16 + b, 8, stride=2), :] = solid * on[b]
        for h in range(2):
            part = chi[pl.ds(pl.multiple_of(x * 16 + h * 8, 8), 8), :]
            scale = 1.0 / (1.0 + part)
            for c in range(3):
                lifted = field[pl.ds(pl.multiple_of((c * 4 + x // 8) * 16 + h * 8, 8), 8), :]
                there = u_ref[c * 32 + x, h * 8 : h * 8 + 8, :]
                out_ref[c * 32 + x, h * 8 : h * 8 + 8, :] = (there + lifted + part * speed_ref[0, c]) * scale
        return carry

    lax.fori_loop(0, 32, plane, 0)


VMEM = pl.BlockSpec(memory_space=pltpu.VMEM)
SMEM = pl.BlockSpec(memory_space=pltpu.SMEM)
LIMIT = 48 * 2**20


def f32(*shape):
    return jax.ShapeDtypeStruct(shape, jnp.float32)


def split(array):
    return array.reshape(2, 3, 256, 128).transpose(1, 2, 0, 3)


def join(array):
    return array.reshape(3, 256, 2, 128).transpose(2, 0, 1, 3).reshape(2, 3, 32768)


def body(vorticity, velocity, level_map, patch_owner, neighbours, fish_slot, fish_mask, fish_speed):
    w, u = split(vorticity), split(velocity)
    ghosts = pl.pallas_call(
        faces_kernel,
        out_shape=f32(576, 128),
        in_specs=[SMEM, VMEM, VMEM],
        out_specs=VMEM,
        scratch_shapes=[
            pltpu.VMEM((576, 128), jnp.float32),
            pltpu.VMEM((1152, 128), jnp.float32),
            pltpu.VMEM((576, 128), jnp.float32),
            pltpu.VMEM((576, 128), jnp.float32),
            pltpu.VMEM((192, 128), jnp.float32),
            pltpu.VMEM((8, 128), jnp.int32),
            pltpu.VMEM((64, 128), jnp.int32),
            pltpu.SemaphoreType.DMA((26,)),
            pltpu.SemaphoreType.DMA((26,)),
        ],
        compiler_params=pltpu.CompilerParams(collective_id=0, has_side_effects=True, vmem_limit_bytes=LIMIT),
        name="faces",
    )(neighbours, w.reshape(1536, 128), u.reshape(1536, 128))
    fold, pick, mean, spread_y, match, spread_z = (jnp.asarray(a) for a in fold_tables())
    fresh, tile = pl.pallas_call(
        stencil_kernel,
        out_shape=(f32(96, 16, 128), f32(8, 128)),
        in_specs=[SMEM, SMEM] + [VMEM] * 6,
        out_specs=(VMEM, VMEM),
        scratch_shapes=[
            pltpu.VMEM((192, 128), jnp.float32),
            pltpu.VMEM((1536, 128), jnp.float32),
            pltpu.VMEM((192, 128), jnp.float32),
            pltpu.VMEM((192, 128), jnp.float32),
        ],
        compiler_params=pltpu.CompilerParams(vmem_limit_bytes=LIMIT),
        name="stencil",
    )(level_map, patch_owner, w.reshape(96, 16, 128), u.reshape(96, 16, 128), ghosts, fold, pick, mean)
    gathered = pl.pallas_call(
        gather_kernel,
        out_shape=f32(256, 512),
        in_specs=[VMEM],
        out_specs=VMEM,
        scratch_shapes=[
            pltpu.VMEM((64, 128), jnp.float32),
            pltpu.VMEM((256, 512), jnp.float32),
            pltpu.SemaphoreType.DMA((17,)),
            pltpu.SemaphoreType.DMA((17,)),
        ],
        compiler_params=pltpu.CompilerParams(collective_id=1, has_side_effects=True, vmem_limit_bytes=LIMIT),
        name="gather",
    )(tile)
    tables = [jnp.asarray(a) for a in dft_tables()]
    moved = pl.pallas_call(
        solve_kernel,
        out_shape=f32(96, 16, 128),
        in_specs=[SMEM] * 3 + [VMEM] * 11,
        out_specs=VMEM,
        scratch_shapes=[pltpu.VMEM((512, 128), jnp.float32), pltpu.VMEM((192, 128), jnp.float32)],
        compiler_params=pltpu.CompilerParams(vmem_limit_bytes=LIMIT),
        name="solve",
    )(patch_owner, fish_slot, fish_speed, fish_mask.reshape(256, 128), u.reshape(96, 16, 128), gathered,
      *tables, spread_y, match, spread_z)
    return join(fresh), join(moved)


def solution(mesh):
    blocks = ("blk", "sub")
    placed = (
        P(blocks, None, None),
        P(blocks, None, None),
        P(blocks),
        P(blocks),
        P(blocks, None),
        P(blocks),
        P(blocks, None),
        P(blocks, None),
    )
    return jax.shard_map(
        body,
        mesh=mesh,
        in_specs=placed,
        out_specs=(P(blocks, None, None), P(blocks, None, None)),
        check_vma=False,
    )
```

```python
import math

import jax
import jax.numpy as jnp
import ml_dtypes
import numpy as np
from jax import lax
from jax.experimental import pallas as pl
from jax.experimental.pallas import tpu as pltpu
from jax.sharding import PartitionSpec as P

MESH = pl.DeviceIdType.MESH
RINGS = 32
GX = 32
GY = 128
GZ = 4


def fold_tables():
    row = np.arange(192)
    lane = np.arange(128)
    n = np.arange(256)
    row_c_ix, row_iy, row_b = row // 16, (row % 16) // 4, row % 2
    lane_iz = (lane % 32) // 8
    live = n < 192
    fold = ((lane_iz[:, None] == n[None, :] % 4) & live[None, :]) * 1.0
    pick = ((n[None, :] // 4 == (row_iy * 12 + row_c_ix)[:, None]) & live[None, :]) * 1.0
    mean = (np.arange(8)[:, None] == row_b[None, :]) / 512.0
    return fold.astype(np.float32), pick.astype(np.float32), mean.astype(np.float32)


def iota(shape, dim):
    return lax.broadcasted_iota(jnp.int32, shape, dim)


def place():
    blk, sub = lax.axis_index("blk"), lax.axis_index("sub")
    return blk // 2, lax.rem(blk, 2), sub


def row_pair(first, second):
    return jnp.where((iota((8, 128), 0) & 1) == 0, first, second)


class Chunk:
    def __init__(self, first, count, s1, r1, s2, r2, sem):
        self.first, self.count = first, count
        self.s1, self.r1, self.s2, self.r2, self.sem = s1, r1, s2, r2, sem
        self.rows = 12 * count

    def at(self, b, f, c):
        return (b * self.count + f - self.first) * 6 + c

    def put(self, b, f, c, plane):
        self.s1[pl.ds(self.at(b, f, c), 8, stride=self.rows), :] = plane

    def own(self, b, f, c):
        return self.s1[pl.ds(self.at(b, f, c), 8, stride=self.rows), :]

    def ghost(self, b, f, c):
        return self.r2[pl.ds(self.at(b, f, c), 8, stride=self.rows), :]

    def piece(self, which, count=1):
        return pl.ds(pl.multiple_of(which * self.rows, 8), count * self.rows)


def front_kernel(nb_ref, level_ref, owner_ref, slot_ref, speed_ref, w_hbm, u_hbm, mask_hbm, fold_hbm, pick_hbm, mean_hbm,
                 fresh_hbm, base_hbm, scale_hbm, g_hbm,
                 wv, uv, solid, fold_ref, pick_ref, mean_ref, out_ref, basis, scales, s1a, r1a, s2a, r2a, s1b, r1b, s2b, r2b,
                 tmp, nbs, nbr, acc, t1, g, in_sem, out_sem, ssem, rsem):
    ring, half, sub = place()
    me = half * 4 + sub
    core = lax.rem(sub, 2)
    y, z = ring // 8, lax.rem(ring, 8)
    wanted_here = ((w_hbm, wv), (u_hbm, uv), (mask_hbm, solid), (fold_hbm, fold_ref), (pick_hbm, pick_ref), (mean_hbm, mean_ref))
    loads = [pltpu.make_async_copy(src, dst, in_sem.at[n]) for n, (src, dst) in enumerate(wanted_here)]
    for load in loads:
        load.start()

    def mate(k):
        other = lax.bitwise_xor(me, k)
        return (ring * 2 + other // 4, lax.rem(other, 4))

    def beside(step):
        return (lax.rem(ring + step + RINGS, RINGS) * 2 + half, sub)

    def along_z(k):
        return ((y * 8 + lax.rem(z + k, 8)) * 2 + half, sub)

    def along_y(k):
        return ((lax.rem(y + k, 4) * 8 + z) * 2 + half, sub)

    mates = [mate(k) for k in range(1, 8)]
    on_z = [along_z(k) for k in range(1, 8)]
    on_y = [along_y(k) for k in range(1, 4)]
    everyone = mates + [beside(1), beside(-1)] + on_z + on_y
    barrier = pltpu.get_barrier_semaphore()
    for device in everyone:
        pl.semaphore_signal(barrier, inc=1, device_id=device, device_id_type=MESH)

    lane = iota((8, 128), 1)
    row = iota((8, 128), 0)
    wants = jnp.zeros((8, 128), jnp.int32)
    for b in range(2):
        for f in range(6):
            wants = jnp.where(lane == b * 6 + f, nb_ref[b, f] + half * 8, wants)
    nbs[...] = wants
    nbr[pl.ds(pl.multiple_of(me * 8, 8), 8), :] = wants
    for load in loads[:2]:
        load.wait()

    flat = (wv.reshape(1536, 128), uv.reshape(1536, 128))

    def source(c):
        return flat[c // 3], (c % 3) * 512

    def remote(src, dst, sem, device):
        return pltpu.make_async_remote_copy(
            src_ref=src, dst_ref=dst, send_sem=ssem.at[sem], recv_sem=rsem.at[sem],
            device_id=device, device_id_type=MESH)

    def start(copies):
        for copy in copies:
            copy.start()
        return copies

    def finish(copies):
        for copy in copies:
            copy.wait()

    xy = Chunk(0, 4, s1a, r1a, s2a, r2a, 8)
    zz = Chunk(4, 2, s1b, r1b, s2b, r2b, 24)

    def scatter_faces(part):
        copies = start([
            remote(part.s1.at[part.piece(lax.bitwise_xor(me, k))], part.r1.at[part.piece(4 + me)], part.sem + k - 1, mate(k))
            for k in range(1, 8)
        ])
        part.r1[part.piece(4 + me), :] = part.s1[part.piece(me), :]
        return copies

    def forward_faces(part):
        return start([
            remote(part.r1.at[part.piece(8, 4)], part.r1.at[part.piece(0, 4)], part.sem + 7, beside(1)),
            remote(part.r1.at[part.piece(4, 4)], part.r1.at[part.piece(12, 4)], part.sem + 8, beside(-1)),
        ])

    def return_faces(part):
        copies = start([
            remote(part.s2.at[part.piece(lax.bitwise_xor(me, k))], part.r2.at[part.piece(me)], part.sem + 8 + k, mate(k))
            for k in range(1, 8)
        ])
        part.r2[part.piece(me), :] = part.s2[part.piece(me), :]
        return copies

    for c in range(6):
        ref, base = source(c)
        for b in range(2):
            for f, x in ((0, 0), (1, 31)):
                xy.put(b, f, c, ref[pl.ds(base + x * 16 + b, 8, stride=2), :])
            low = high = jnp.zeros((8, 128), jnp.float32)
            for n in range(4):
                first = ref[pl.ds(base + n * 128 + b, 8, stride=16), :]
                last = ref[pl.ds(base + n * 128 + 14 + b, 8, stride=16), :]
                if n:
                    first = pltpu.roll(first, 32 * n, 1)
                if n != 3:
                    last = pltpu.roll(last, (32 * n + 32) % 128, 1)
                here = lane // 32 == n
                low = jnp.where(here, first, low)
                high = jnp.where(here, last, high)
            xy.put(b, 2, c, low)
            xy.put(b, 3, c, high)

    pl.semaphore_wait(barrier, len(everyone))
    mine = pl.ds(pl.multiple_of(me * 8, 8), 8)
    sent_wants = start([remote(nbs, nbr.at[mine], k - 1, mate(k)) for k in range(1, 8)])
    sent_xy = scatter_faces(xy)

    def gather_z(x, held):
        at_low = (lane & 31) == x
        at_high = (lane & 31) == ((x + 31) & 31)
        fresh = []
        for c in range(6):
            ref, base = source(c)
            for h in range(2):
                plane = ref[pl.ds(pl.multiple_of(base + x * 16 + h * 8, 8), 8), :]
                turned = pltpu.roll(plane, x, 1)
                low, high = held[(c * 2 + h) * 2], held[(c * 2 + h) * 2 + 1]
                fresh += [jnp.where(at_low, turned, low), jnp.where(at_high, turned, high)]
        return tuple(fresh)

    zero = jnp.zeros((8, 128), jnp.float32)
    packed = lax.fori_loop(0, 32, gather_z, (zero,) * 24)
    for c in range(6):
        for which in range(2):
            for h in range(2):
                at = (c * 2 + which) * 16 + h * 8
                plane = packed[(c * 2 + h) * 2 + which]
                tmp[at : at + 8, :] = pltpu.roll(plane, 97, 1) if which else plane
    for c in range(6):
        for which in range(2):
            for b in range(2):
                zz.put(b, 4 + which, c, tmp[pl.ds((c * 2 + which) * 16 + b, 8, stride=2), :])
    sent_zz = scatter_faces(zz)

    def scale(level):
        return lax.shift_left(1, level).astype(jnp.float32)

    sizes = [scale(level_ref[b]) for b in range(2)]
    slopes_of = [0.05 * 0.5 * size for size in sizes]
    spread_of = [0.05 * 0.1 * (size * size) for size in sizes]
    slope = row_pair(*slopes_of)
    spread = row_pair(*spread_of)

    def around(x, c, h):
        ref = (wv, uv)[c // 3]
        at = (c % 3) * 32 + x
        rows = slice(h * 8, h * 8 + 8)
        here = ref[at, rows, :]
        left = jnp.zeros_like(here) if isinstance(x, int) and x == 0 else ref[at - 1, rows, :]
        right = jnp.zeros_like(here) if isinstance(x, int) and x == 31 else ref[at + 1, rows, :]
        if h == 0:
            before = jnp.where(row < 2, 0.0, pltpu.roll(here, 2, 0))
            after = ref[at, 2:10, :]
        else:
            before = ref[at, 6:14, :]
            after = jnp.where(row >= 6, 0.0, pltpu.roll(here, 6, 0))
        before = pltpu.roll(jnp.where(lane >= 96, before, here), 32, 1)
        after = pltpu.roll(jnp.where(lane < 32, after, here), 96, 1)
        below = jnp.where((lane & 31) == 0, 0.0, pltpu.roll(here, 1, 1))
        above = jnp.where((lane & 31) == 31, 0.0, pltpu.roll(here, 127, 1))
        return here, (left, right), (before, after), (below, above)

    def plane(x):
        for h in range(2):
            parts = [around(x, c, h) for c in range(6)]
            heres = [part[0] for part in parts]
            slopes = [[part[1 + d][1] - part[1 + d][0] for d in range(3)] for part in parts]
            for i in range(3):
                turn = heres[0] * slopes[3 + i][0] + heres[1] * slopes[3 + i][1] + heres[2] * slopes[3 + i][2]
                turn -= heres[3] * slopes[i][0] + heres[4] * slopes[i][1] + heres[5] * slopes[i][2]
                ends = [part for d in range(3) for part in parts[i][1 + d]]
                total = (ends[0] + ends[1]) + (ends[2] + ends[3]) + (ends[4] + ends[5])
                out_ref[i * 32 + x, h * 8 : h * 8 + 8, :] = (
                    heres[i] + slope * turn + spread * (total - 6.0 * heres[i])
                )

    def planes(low, high):
        def step(x, carry):
            plane(x)
            return carry

        lax.fori_loop(low, high, step, 0)

    plane(0)
    planes(1, 15)
    finish(sent_wants)
    finish(sent_xy)
    sent_xy = forward_faces(xy)
    planes(15, 23)
    finish(sent_zz)
    sent_zz = forward_faces(zz)
    planes(23, 31)
    plane(31)

    slot = iota((8, 32), 1)
    dead_low = (ring == 0).astype(jnp.int32)
    dead_high = (ring == RINGS - 1).astype(jnp.int32)
    alive = 1 - dead_low * (slot < 8).astype(jnp.int32) - dead_high * (slot >= 24).astype(jnp.int32)
    alive = alive.astype(jnp.float32)

    def select(part):
        wanted = nbr[pl.ds(0, 8, stride=8), :]
        for f in range(part.first, part.first + part.count):
            hot = jnp.concatenate(
                [jnp.where(wanted[:, b * 6 + f : b * 6 + f + 1] == slot, alive, 0.0) for b in range(2)], axis=0)
            data = jnp.concatenate(
                [part.r1[pl.ds(part.at(0, f ^ 1, c), 32, stride=6 * part.count), :] for c in range(6)], axis=1)
            hot = hot.astype(jnp.bfloat16)
            got = sum(dot(hot, third) for third in thirds(data))
            for b in range(2):
                for c in range(6):
                    part.s2[pl.ds(part.at(b, f, c), 8, stride=part.rows), :] = (
                        got[b * 8 : b * 8 + 8, c * 128 : c * 128 + 128]
                    )

    finish(sent_xy)
    select(xy)
    sent_xy = return_faces(xy)
    finish(sent_zz)
    select(zz)
    sent_zz = return_faces(zz)

    moved = out_ref.reshape(1536, 128)

    def added(part, b, f):
        ghosts = [part.ghost(b, f, c) for c in range(6)]
        vort, veloc = part.own(b, f, f // 2), part.own(b, f, 3 + f // 2)
        sign = slopes_of[b] * (1.0 if f % 2 else -1.0)
        vort, veloc = vort * sign, spread_of[b] - veloc * sign
        return [vort * ghosts[3 + i] + veloc * ghosts[i] for i in range(3)]

    finish(sent_xy)
    for b in range(2):
        for f, x in ((0, 0), (1, 31)):
            for i, extra in enumerate(added(xy, b, f)):
                moved[pl.ds(i * 512 + x * 16 + b, 8, stride=2), :] += extra
        for f, at, zone in ((2, 0, 0), (3, 14, 3)):
            for i, extra in enumerate(added(xy, b, f)):
                for n in range(4):
                    turn = (32 * (zone - n)) % 128
                    part = pltpu.roll(extra, turn, 1) if turn else extra
                    moved[pl.ds(i * 512 + n * 128 + at + b, 8, stride=16), :] += jnp.where(lane // 32 == zone, part, 0.0)
    finish(sent_zz)
    for b in range(2):
        for which in range(2):
            for i, extra in enumerate(added(zz, b, 4 + which)):
                tmp[pl.ds((i * 2 + which) * 16 + b, 8, stride=2), :] = extra
    ends = [[tmp[n * 16 + h * 8 : n * 16 + h * 8 + 8, :] for h in range(2)] for n in range(6)]

    def close(ix, carry):
        sums = [jnp.zeros((8, 128), jnp.float32)] * 6
        for step in range(8):
            x = ix * 8 + step
            for i in range(3):
                for h in range(2):
                    low = pltpu.roll(ends[i * 2][h], (128 - x) & 127, 1)
                    high = pltpu.roll(ends[i * 2 + 1][h], (159 - x) & 127, 1)
                    extra = jnp.where((lane & 31) == 0, low, jnp.where((lane & 31) == 31, high, 0.0))
                    fresh = out_ref[i * 32 + x, h * 8 : h * 8 + 8, :] + extra
                    out_ref[i * 32 + x, h * 8 : h * 8 + 8, :] = fresh
                    sums[i * 2 + h] = sums[i * 2 + h] + fresh
        for i in range(3):
            for h in range(2):
                acc[pl.ds(pl.multiple_of((i * 4 + ix) * 16 + h * 8, 8), 8), :] = sums[i * 2 + h]
        return carry

    lax.fori_loop(0, 4, close, 0)

    stores = [pltpu.make_async_copy(out_ref, fresh_hbm, out_sem.at[0])]
    stores[0].start()
    for load in loads[2:]:
        load.wait()
    fold, mean = fold_ref[...].astype(jnp.bfloat16), mean_ref[...].astype(jnp.bfloat16)
    folded = sum(dot(part, fold) for part in thirds(acc[...])) * pick_ref[...]
    rows = sum(dot(mean, part) for part in thirds(folded))
    wide_row, wide_lane = iota((8, 256), 0), iota((8, 256), 1)

    def shrink(level):
        return jnp.where(level == 0, 1.0, jnp.where(level == 1, 0.125, 0.015625))

    rows = rows * jnp.where(wide_row == 0, shrink(level_ref[0]), shrink(level_ref[1]))
    owners = jnp.where(wide_row == 0, owner_ref[0], owner_ref[1]).astype(jnp.float32)
    rows = jnp.where(wide_lane == 192, owners, rows)
    gap = jnp.zeros((2, 128), jnp.float32)
    spot = half * 2 + sub // 2
    mine = pl.ds(pl.multiple_of(spot * 8, 8), 8)
    t1[mine, :] = jnp.concatenate(
        [rows[0:1, 0:128], rows[0:1, 128:256], gap, rows[1:2, 0:128], rows[1:2, 128:256], gap], axis=0)

    def share(ref, targets, first):
        return start([remote(ref, ref, first + n, device) for n, device in enumerate(targets)])

    sent = share(t1.at[mine], [mates[k - 1] for k in (2, 4, 6)], 40)

    on = [jnp.where(slot_ref[0] == b, 10.0, 0.0) for b in range(2)]
    flat_scale = scales.reshape(512, 128)

    def penalise(x, carry):
        part = solid[pl.ds(pl.multiple_of(x * 8, 8), 8), :]
        for b in range(2):
            flat_scale[pl.ds(x * 16 + b, 8, stride=2), :] = part * on[b]
        for h in range(2):
            rows = slice(h * 8, h * 8 + 8)
            chi = scales[x, rows, :]
            scale = 1.0 / (1.0 + chi)
            scales[x, rows, :] = scale
            for c in range(3):
                basis[c * 32 + x, rows, :] = (uv[c * 32 + x, rows, :] + chi * speed_ref[0, c]) * scale
        return carry

    lax.fori_loop(0, 32, penalise, 0)
    stores += start([
        pltpu.make_async_copy(basis, base_hbm, out_sem.at[1]),
        pltpu.make_async_copy(scales, scale_hbm, out_sem.at[2]),
    ])
    finish(sent)
    first = core * 256
    at = pl.ds(pl.multiple_of(first + ring * 8, 8), 8)
    for t in range(2):
        g[at, t * 128 : t * 128 + 128] = t1[pl.ds(t, 8, stride=4), :]
    finish(share(g.at[at], on_z, 43))
    finish(share(g.at[pl.ds(pl.multiple_of(first + y * 64, 64), 64)], on_y, 50))
    own_half = pl.ds(pl.multiple_of(first, 256), 256)
    other_half = pl.ds(pl.multiple_of(256 - first, 256), 256)
    sent = share(g.at[own_half], [mates[0]], 53)
    stores += start([pltpu.make_async_copy(g.at[own_half], g_hbm.at[own_half], out_sem.at[3])])
    finish(sent)
    stores += start([pltpu.make_async_copy(g.at[other_half], g_hbm.at[other_half], out_sem.at[4])])
    finish(stores)


def halves(table):
    high = table.astype(ml_dtypes.bfloat16).astype(np.float64)
    low = (table - high).astype(ml_dtypes.bfloat16).astype(np.float64)
    return high, low


def solve_tables():
    space = np.arange(128)
    px, ix, iz = space // 16, (space // 4) % 4, space % 4
    x, z = 4 * px + ix, iz
    kx, kz = space // 4, space % 4
    iy, py = space // 32, space % 32
    y = 4 * py + iy
    ky = space
    theta = 2.0 * np.pi * ((kx[:, None] * x[None, :] % 32) / 32.0 + (kz[:, None] * z[None, :] % 4) / 4.0)
    phi = 2.0 * np.pi * ((y[:, None] * ky[None, :]) % 128) / 128.0
    high, low = halves(np.concatenate([np.cos(phi), -np.sin(phi)], axis=1))
    fwd_y = np.concatenate([high, high, low], axis=0)
    high, low = halves(np.concatenate([np.cos(theta), np.sin(theta)], axis=0))
    fwd_xz = np.concatenate([high, low], axis=1)
    inv_xz = np.concatenate([np.cos(theta.T), np.sin(theta.T)], axis=0).astype(np.float32)
    line = np.arange(256)
    turn = 2.0 * np.pi * (((4 * (line // 8) + (line % 8) // 2)[:, None] * ky[None, :]) % 128) / 128.0
    inv_y = (np.concatenate([np.cos(turn), -np.sin(turn)], axis=1) / 16384.0).astype(np.float32)

    def waves(index, length):
        signed = np.where(index < (length + 1) // 2, index, index - length)
        full = signed * (2.0 * math.pi / length)
        return full, np.where(index == length // 2, 0.0, full)

    full_x, slope_x = waves(kx, GX)
    full_y, slope_y = waves(ky, GY)
    full_z, slope_z = waves(kz, GZ)
    square = (full_x**2 + full_z**2)[:, None] + (full_y**2)[None, :]
    inverse = np.where(square > 0, 1.0 / np.where(square > 0, square, 1.0), 0.0)
    spectral = np.concatenate([inverse * slope_x[:, None], inverse * slope_y[None, :], inverse * slope_z[:, None]])
    src = np.arange(96)
    row = np.arange(192)
    src_c, src_b, src_ix, src_iz = src // 32, (src // 16) % 2, (src // 4) % 4, src % 4
    match = ((src_c * 4 + src_ix)[None, :] == (row // 16)[:, None]) & (src_b[None, :] == (row % 2)[:, None])
    spread_z = src_iz[:, None] == ((np.arange(128) % 32) // 8)[None, :]
    return tuple(a.astype(np.float32) for a in (inv_xz, inv_y, fwd_y, fwd_xz, spectral, match * 1.0, spread_z * 1.0))


def cut(array):
    high = array.astype(jnp.bfloat16)
    return high, (array - high.astype(jnp.float32)).astype(jnp.bfloat16)


def thirds(array):
    high = array.astype(jnp.bfloat16)
    rest = array - high.astype(jnp.float32)
    middle = rest.astype(jnp.bfloat16)
    return high, middle, (rest - middle.astype(jnp.float32)).astype(jnp.bfloat16)


def dot(left, right):
    return jnp.dot(left, right, preferred_element_type=jnp.float32)


def dot_nt(left, right):
    return lax.dot_general(left, right, (((1,), (1,)), ((), ())), preferred_element_type=jnp.float32)


def solve(owners, ready, g_ref, inv_xz, inv_y, fwd_y, fwd_xz, spectral, match, spread_z, near_y):
    ready(0)
    sent = g_ref[...]
    hot = (sent[:, 192:193] == iota((512, 256), 1).astype(jnp.float32)).astype(jnp.bfloat16)
    high, low = cut(sent.T)
    columns = dot(high, hot) + dot(low, hot)
    ready(1)
    ready(2)
    for b in range(2):
        rows = pl.ds(pl.multiple_of((owners[b] % 32) * 8, 8), 8)
        for n in range(2):
            near_y[pl.ds(n * 16 + b, 8, stride=2), :] = inv_y[rows, n * 128 : n * 128 + 128]
    near_high, near_low = cut(jnp.concatenate([near_y[0:16, :], near_y[16:32, :]], axis=1))
    chosen_high, chosen_low = cut(jnp.concatenate(
        [
            inv_xz[pl.ds(pl.multiple_of(side * 128 + (owner // 32) * 16, 16), 16), :]
            for side in range(2)
            for owner in owners
        ],
        axis=0,
    ))
    lane = iota((48, 128), 1)
    rows = []
    for px in range(8):
        held = None
        for iy in range(4):
            part = columns[iy * 48 : iy * 48 + 48, (px // 4) * 128 : (px // 4) * 128 + 128]
            turn = ((iy - px % 4) * 32) % 128
            if turn:
                part = pltpu.roll(part, turn, 1)
            held = part if held is None else jnp.where(lane >= iy * 32, part, held)
        rows.append(held)
    high, low = cut(jnp.concatenate(rows, axis=0))
    ready(3)
    table = fwd_y[...].astype(jnp.bfloat16)
    waves_y = dot(jnp.concatenate([high, low], axis=1), table[0:256]) + dot(high, table[256:384])
    stacked = jnp.concatenate(
        [
            jnp.concatenate([waves_y[px * 48 + c * 16 : px * 48 + c * 16 + 16, :] for px in range(8)], axis=0)
            for c in range(3)
        ],
        axis=1,
    )
    high, low = cut(stacked)
    ready(4)
    table = fwd_xz[...].astype(jnp.bfloat16)
    full = dot(table, jnp.concatenate([high, high], axis=0)) + dot(table[:, 0:128], low)
    for n in range(5, 8):
        ready(n)
    slope_x, slope_y, slope_z = spectral[0:128, :], spectral[128:256, :], spectral[256:384, :]
    real, imag = [], []
    for c in range(3):
        low = full[:, c * 256 : c * 256 + 128]
        high = full[:, c * 256 + 128 : c * 256 + 256]
        real.append(low[0:128] + high[128:256])
        imag.append(high[0:128] - low[128:256])

    def cross(hat):
        return [
            slope_y * hat[2] - slope_z * hat[1],
            slope_z * hat[0] - slope_x * hat[2],
            slope_x * hat[1] - slope_y * hat[0],
        ]

    cross_real, cross_imag = cross(real), cross(imag)
    high, low = cut(jnp.concatenate([part for c in range(3) for part in (-cross_imag[c], cross_real[c])], axis=1))
    near = dot(jnp.concatenate([chosen_high, chosen_low], axis=1), jnp.concatenate([high, high], axis=0))
    near = near + dot(chosen_high, low)
    lines = []
    for c in range(3):
        low = near[:, c * 256 : c * 256 + 128]
        high = near[:, c * 256 + 128 : c * 256 + 256]
        lines.append(jnp.concatenate([low[0:32] - high[32:64], high[0:32] + low[32:64]], axis=1))
    high, low = cut(jnp.concatenate(lines, axis=0))
    turned = dot_nt(near_high, high) + (dot_nt(near_high, low) + dot_nt(near_low, high))
    high, low = cut(jnp.concatenate([turned] * 12, axis=0) * match[...])
    table = spread_z[...].astype(jnp.bfloat16)
    return dot(high, table) + dot(low, table)


def solve_kernel(owner_ref, *refs):
    sources, (fresh_out, out_hbm), refs = refs[:11], refs[11:13], refs[13:]
    held, (near_y, field, moved, sem, out_sem) = refs[:11], refs[11:]
    loads = [pltpu.make_async_copy(src, dst, sem.at[n]) for n, (src, dst) in enumerate(zip(sources, held))]
    for load in loads:
        load.start()
    base, scale, fresh = held[8:]
    owners = (owner_ref[0], owner_ref[1])
    stores = [pltpu.make_async_copy(fresh, fresh_out, out_sem.at[12])]

    def ready(n):
        loads[n].wait()
        if n == 7:
            loads[10].wait()
            stores[0].start()

    field[...] = solve(owners, ready, *held[:8], near_y)
    for load in loads[8:10]:
        load.wait()
    for ix in range(4):
        lifted = [[field[(c * 4 + ix) * 16 + h * 8 : (c * 4 + ix) * 16 + h * 8 + 8, :] for h in range(2)] for c in range(3)]
        for x in range(ix * 8, ix * 8 + 8):
            for h in range(2):
                rows = slice(h * 8, h * 8 + 8)
                part = scale[x, rows, :]
                for c in range(3):
                    moved[c * 32 + x, rows, :] = base[c * 32 + x, rows, :] + lifted[c][h] * part
        for c in range(3):
            planes = pl.ds(c * 32 + ix * 8, 8)
            stores.append(pltpu.make_async_copy(moved.at[planes], out_hbm.at[planes], out_sem.at[ix * 3 + c]))
            stores[-1].start()
    for copy in stores:
        copy.wait()


VMEM = pl.BlockSpec(memory_space=pltpu.VMEM)
SMEM = pl.BlockSpec(memory_space=pltpu.SMEM)
ANY = pl.BlockSpec(memory_space=pl.ANY)
LIMIT = 62 * 2**20


def f32(*shape):
    return jax.ShapeDtypeStruct(shape, jnp.float32)


def scratch(*shape):
    return pltpu.VMEM(shape, jnp.float32)


def split(array):
    return array.reshape(2, 3, 256, 128).transpose(1, 2, 0, 3)


def join(array):
    return array.reshape(3, 256, 2, 128).transpose(2, 0, 1, 3).reshape(2, 3, 32768)


def body(vorticity, velocity, level_map, patch_owner, neighbours, fish_slot, fish_mask, fish_speed):
    w, u = split(vorticity), split(velocity)
    w, u = w.reshape(96, 16, 128), u.reshape(96, 16, 128)
    field = f32(96, 16, 128)

    def faces(count):
        return [scratch(rows * count, 128) for rows in (96, 192, 96, 96)]

    fresh, base, scale, gathered = pl.pallas_call(
        front_kernel,
        out_shape=(field, field, f32(32, 16, 128), f32(512, 256)),
        in_specs=[SMEM] * 5 + [ANY] * 6,
        out_specs=(ANY,) * 4,
        scratch_shapes=[
            scratch(96, 16, 128),
            scratch(96, 16, 128),
            scratch(256, 128),
            scratch(128, 256),
            scratch(192, 256),
            scratch(8, 192),
            scratch(96, 16, 128),
            scratch(96, 16, 128),
            scratch(32, 16, 128),
            *faces(4),
            *faces(2),
            scratch(192, 128),
            pltpu.VMEM((8, 128), jnp.int32),
            pltpu.VMEM((64, 128), jnp.int32),
            scratch(192, 128),
            scratch(32, 128),
            scratch(512, 256),
            pltpu.SemaphoreType.DMA((6,)),
            pltpu.SemaphoreType.DMA((5,)),
            pltpu.SemaphoreType.DMA((56,)),
            pltpu.SemaphoreType.DMA((56,)),
        ],
        compiler_params=pltpu.CompilerParams(collective_id=0, has_side_effects=True, vmem_limit_bytes=LIMIT),
        name="front",
    )(neighbours, level_map, patch_owner, fish_slot, fish_speed, w, u, fish_mask.reshape(256, 128),
      *(jnp.asarray(a) for a in fold_tables()))
    sources = (gathered, *(jnp.asarray(a) for a in solve_tables()), base, scale, fresh)
    fresh, moved = pl.pallas_call(
        solve_kernel,
        out_shape=(field, field),
        in_specs=[SMEM] + [ANY] * 11,
        out_specs=(ANY, ANY),
        scratch_shapes=[
            *(scratch(*array.shape) for array in sources),
            scratch(32, 128),
            scratch(192, 128),
            scratch(96, 16, 128),
            pltpu.SemaphoreType.DMA((11,)),
            pltpu.SemaphoreType.DMA((13,)),
        ],
        compiler_params=pltpu.CompilerParams(vmem_limit_bytes=LIMIT),
        name="solve",
    )(patch_owner, *sources)
    return join(fresh), join(moved)


def solution(mesh):
    blocks = ("blk", "sub")
    placed = (
        P(blocks, None, None),
        P(blocks, None, None),
        P(blocks),
        P(blocks),
        P(blocks, None),
        P(blocks),
        P(blocks, None),
        P(blocks, None),
    )
    return jax.shard_map(
        body,
        mesh=mesh,
        in_specs=placed,
        out_specs=(P(blocks, None, None), P(blocks, None, None)),
        check_vma=False,
    )
```

```python
import math

import jax
import jax.numpy as jnp
import ml_dtypes
import numpy as np
from jax import lax
from jax.experimental import pallas as pl
from jax.experimental.pallas import tpu as pltpu
from jax.sharding import PartitionSpec as P

MESH = pl.DeviceIdType.MESH
RINGS = 32
GX = 32
GY = 128
GZ = 4


def fold_tables():
    row = np.arange(192)
    lane = np.arange(128)
    n = np.arange(256)
    row_c_ix, row_iy, row_b = row // 16, (row % 16) // 4, row % 2
    lane_iz = (lane % 32) // 8
    live = n < 192
    fold = ((lane_iz[:, None] == n[None, :] % 4) & live[None, :]) * 1.0
    pick = ((n[None, :] // 4 == (row_iy * 12 + row_c_ix)[:, None]) & live[None, :]) * 1.0
    mean = (np.arange(8)[:, None] == row_b[None, :]) / 512.0
    return fold.astype(np.float32), pick.astype(np.float32), mean.astype(np.float32)


def iota(shape, dim):
    return lax.broadcasted_iota(jnp.int32, shape, dim)


def place():
    blk, sub = lax.axis_index("blk"), lax.axis_index("sub")
    return blk // 2, lax.rem(blk, 2), sub


def row_pair(first, second):
    return jnp.where((iota((8, 128), 0) & 1) == 0, first, second)


class Chunk:
    def __init__(self, first, count, s1, r1, s2, r2, sem):
        self.first, self.count = first, count
        self.s1, self.r1, self.s2, self.r2, self.sem = s1, r1, s2, r2, sem
        self.rows = 12 * count

    def at(self, b, f, c):
        return (b * self.count + f - self.first) * 6 + c

    def put(self, b, f, c, plane):
        self.s1[pl.ds(self.at(b, f, c), 8, stride=self.rows), :] = plane

    def own(self, b, f, c):
        return self.s1[pl.ds(self.at(b, f, c), 8, stride=self.rows), :]

    def ghost(self, b, f, c):
        return self.r2[pl.ds(self.at(b, f, c), 8, stride=self.rows), :]

    def piece(self, which, count=1):
        return pl.ds(pl.multiple_of(which * self.rows, 8), count * self.rows)


def front_kernel(nb_ref, level_ref, owner_ref, speed_ref, slot_hbm, *refs):
    sources, (fresh_hbm, both_hbm, field_hbm), refs = refs[:13], refs[13:16], refs[16:]
    held, refs = refs[:13], refs[13:]
    wv, uv, solid, fold_ref, pick_ref, mean_ref, inv_xz, inv_y, fwd_y, fwd_xz, spectral, match, spread_z = held
    (out_ref, both, field, s1a, r1a, s2a, r2a, s1b, r1b, s2b, r2b, tmp, nbs, nbr, acc, t1, g, chosen, near_y, mine_s, peer_s,
     slot_ref, in_sem, out_sem, ssem, rsem) = refs
    ring, half, sub = place()
    me = half * 4 + sub
    y, z = ring // 8, lax.rem(ring, 8)
    loads = [pltpu.make_async_copy(src, dst, in_sem.at[n]) for n, (src, dst) in enumerate(zip(sources, held))]
    loads.append(pltpu.make_async_copy(slot_hbm, slot_ref, in_sem.at[13]))
    for load in loads:
        load.start()

    def mate(k):
        other = lax.bitwise_xor(me, k)
        return (ring * 2 + other // 4, lax.rem(other, 4))

    def beside(step):
        return (lax.rem(ring + step + RINGS, RINGS) * 2 + half, sub)

    def along_z(k):
        return ((y * 8 + lax.rem(z + k, 8)) * 2 + half, sub)

    def along_y(k):
        return ((lax.rem(y + k, 4) * 8 + z) * 2 + half, sub)

    mates = [mate(k) for k in range(1, 8)]
    on_z = [along_z(k) for k in range(1, 8)]
    on_y = [along_y(k) for k in range(1, 4)]
    everyone = mates + [beside(1), beside(-1)] + on_z + on_y
    barrier = pltpu.get_barrier_semaphore()
    for device in everyone:
        pl.semaphore_signal(barrier, inc=1, device_id=device, device_id_type=MESH)

    lane = iota((8, 128), 1)
    row = iota((8, 128), 0)
    wants = jnp.zeros((8, 128), jnp.int32)
    for b in range(2):
        for f in range(6):
            wants = jnp.where(lane == b * 6 + f, nb_ref[b, f] + half * 8, wants)
        wants = jnp.where(lane == 12 + b, owner_ref[b], wants)
    nbs[...] = wants
    nbr[pl.ds(pl.multiple_of(me * 8, 8), 8), :] = wants
    for load in loads[:2]:
        load.wait()

    flat = (wv.reshape(1536, 128), uv.reshape(1536, 128))

    def source(c):
        return flat[c // 3], (c % 3) * 512

    def remote(src, dst, sem, device):
        return pltpu.make_async_remote_copy(
            src_ref=src, dst_ref=dst, send_sem=ssem.at[sem], recv_sem=rsem.at[sem],
            device_id=device, device_id_type=MESH)

    def start(copies):
        for copy in copies:
            copy.start()
        return copies

    def finish(copies):
        for copy in copies:
            copy.wait()

    xy = Chunk(0, 4, s1a, r1a, s2a, r2a, 8)
    zz = Chunk(4, 2, s1b, r1b, s2b, r2b, 24)

    def scatter_faces(part):
        copies = start([
            remote(part.s1.at[part.piece(lax.bitwise_xor(me, k))], part.r1.at[part.piece(4 + me)], part.sem + k - 1, mate(k))
            for k in range(1, 8)
        ])
        part.r1[part.piece(4 + me), :] = part.s1[part.piece(me), :]
        return copies

    def forward_faces(part):
        return start([
            remote(part.r1.at[part.piece(8, 4)], part.r1.at[part.piece(0, 4)], part.sem + 7, beside(1)),
            remote(part.r1.at[part.piece(4, 4)], part.r1.at[part.piece(12, 4)], part.sem + 8, beside(-1)),
        ])

    def return_faces(part):
        copies = start([
            remote(part.s2.at[part.piece(lax.bitwise_xor(me, k))], part.r2.at[part.piece(me)], part.sem + 8 + k, mate(k))
            for k in range(1, 8)
        ])
        part.r2[part.piece(me), :] = part.s2[part.piece(me), :]
        return copies

    for c in range(6):
        ref, base = source(c)
        for b in range(2):
            for f, x in ((0, 0), (1, 31)):
                xy.put(b, f, c, ref[pl.ds(base + x * 16 + b, 8, stride=2), :])
            low = high = jnp.zeros((8, 128), jnp.float32)
            for n in range(4):
                first = ref[pl.ds(base + n * 128 + b, 8, stride=16), :]
                last = ref[pl.ds(base + n * 128 + 14 + b, 8, stride=16), :]
                if n:
                    first = pltpu.roll(first, 32 * n, 1)
                if n != 3:
                    last = pltpu.roll(last, (32 * n + 32) % 128, 1)
                here = lane // 32 == n
                low = jnp.where(here, first, low)
                high = jnp.where(here, last, high)
            xy.put(b, 2, c, low)
            xy.put(b, 3, c, high)

    pl.semaphore_wait(barrier, len(everyone))
    mine = pl.ds(pl.multiple_of(me * 8, 8), 8)
    sent_wants = start([remote(nbs, nbr.at[mine], k - 1, mate(k)) for k in range(1, 8)])
    sent_xy = scatter_faces(xy)

    def gather_z(x, held):
        at_low = (lane & 31) == x
        at_high = (lane & 31) == ((x + 31) & 31)
        fresh = []
        for c in range(6):
            ref, base = source(c)
            for h in range(2):
                plane = ref[pl.ds(pl.multiple_of(base + x * 16 + h * 8, 8), 8), :]
                turned = pltpu.roll(plane, x, 1)
                low, high = held[(c * 2 + h) * 2], held[(c * 2 + h) * 2 + 1]
                fresh += [jnp.where(at_low, turned, low), jnp.where(at_high, turned, high)]
        return tuple(fresh)

    zero = jnp.zeros((8, 128), jnp.float32)
    packed = lax.fori_loop(0, 32, gather_z, (zero,) * 24)
    for c in range(6):
        for which in range(2):
            for h in range(2):
                at = (c * 2 + which) * 16 + h * 8
                plane = packed[(c * 2 + h) * 2 + which]
                tmp[at : at + 8, :] = pltpu.roll(plane, 97, 1) if which else plane
    for c in range(6):
        for which in range(2):
            for b in range(2):
                zz.put(b, 4 + which, c, tmp[pl.ds((c * 2 + which) * 16 + b, 8, stride=2), :])
    sent_zz = scatter_faces(zz)

    def scale(level):
        return lax.shift_left(1, level).astype(jnp.float32)

    sizes = [scale(level_ref[b]) for b in range(2)]
    slopes_of = [0.05 * 0.5 * size for size in sizes]
    spread_of = [0.05 * 0.1 * (size * size) for size in sizes]
    slope = row_pair(*slopes_of)
    spread = row_pair(*spread_of)

    def around(x, c, h):
        ref = (wv, uv)[c // 3]
        at = (c % 3) * 32 + x
        rows = slice(h * 8, h * 8 + 8)
        here = ref[at, rows, :]
        left = jnp.zeros_like(here) if isinstance(x, int) and x == 0 else ref[at - 1, rows, :]
        right = jnp.zeros_like(here) if isinstance(x, int) and x == 31 else ref[at + 1, rows, :]
        if h == 0:
            before = jnp.where(row < 2, 0.0, pltpu.roll(here, 2, 0))
            after = ref[at, 2:10, :]
        else:
            before = ref[at, 6:14, :]
            after = jnp.where(row >= 6, 0.0, pltpu.roll(here, 6, 0))
        before = pltpu.roll(jnp.where(lane >= 96, before, here), 32, 1)
        after = pltpu.roll(jnp.where(lane < 32, after, here), 96, 1)
        below = jnp.where((lane & 31) == 0, 0.0, pltpu.roll(here, 1, 1))
        above = jnp.where((lane & 31) == 31, 0.0, pltpu.roll(here, 127, 1))
        return here, (left, right), (before, after), (below, above)

    def plane(x):
        for h in range(2):
            parts = [around(x, c, h) for c in range(6)]
            heres = [part[0] for part in parts]
            slopes = [[part[1 + d][1] - part[1 + d][0] for d in range(3)] for part in parts]
            for i in range(3):
                turn = heres[0] * slopes[3 + i][0] + heres[1] * slopes[3 + i][1] + heres[2] * slopes[3 + i][2]
                turn -= heres[3] * slopes[i][0] + heres[4] * slopes[i][1] + heres[5] * slopes[i][2]
                ends = [part for d in range(3) for part in parts[i][1 + d]]
                total = (ends[0] + ends[1]) + (ends[2] + ends[3]) + (ends[4] + ends[5])
                out_ref[i * 32 + x, h * 8 : h * 8 + 8, :] = (
                    heres[i] + slope * turn + spread * (total - 6.0 * heres[i])
                )

    def planes(low, high):
        def step(x, carry):
            plane(x)
            return carry

        lax.fori_loop(low, high, step, 0)

    plane(0)
    planes(1, 15)
    finish(sent_wants)
    finish(sent_xy)
    sent_xy = forward_faces(xy)
    planes(15, 23)
    finish(sent_zz)
    sent_zz = forward_faces(zz)
    planes(23, 31)
    plane(31)

    slot = iota((8, 32), 1)
    dead_low = (ring == 0).astype(jnp.int32)
    dead_high = (ring == RINGS - 1).astype(jnp.int32)
    alive = 1 - dead_low * (slot < 8).astype(jnp.int32) - dead_high * (slot >= 24).astype(jnp.int32)
    alive = alive.astype(jnp.float32)

    def select(part):
        wanted = nbr[pl.ds(0, 8, stride=8), :]
        for f in range(part.first, part.first + part.count):
            hot = jnp.concatenate(
                [jnp.where(wanted[:, b * 6 + f : b * 6 + f + 1] == slot, alive, 0.0) for b in range(2)], axis=0)
            data = jnp.concatenate(
                [part.r1[pl.ds(part.at(0, f ^ 1, c), 32, stride=6 * part.count), :] for c in range(6)], axis=1)
            hot = hot.astype(jnp.bfloat16)
            got = sum(dot(hot, third) for third in thirds(data))
            for b in range(2):
                for c in range(6):
                    part.s2[pl.ds(part.at(b, f, c), 8, stride=part.rows), :] = (
                        got[b * 8 : b * 8 + 8, c * 128 : c * 128 + 128]
                    )

    finish(sent_xy)
    select(xy)
    sent_xy = return_faces(xy)
    finish(sent_zz)
    select(zz)
    sent_zz = return_faces(zz)

    moved = out_ref.reshape(1536, 128)

    def added(part, b, f):
        ghosts = [part.ghost(b, f, c) for c in range(6)]
        vort, veloc = part.own(b, f, f // 2), part.own(b, f, 3 + f // 2)
        sign = slopes_of[b] * (1.0 if f % 2 else -1.0)
        vort, veloc = vort * sign, spread_of[b] - veloc * sign
        return [vort * ghosts[3 + i] + veloc * ghosts[i] for i in range(3)]

    finish(sent_xy)
    for b in range(2):
        for f, x in ((0, 0), (1, 31)):
            for i, extra in enumerate(added(xy, b, f)):
                moved[pl.ds(i * 512 + x * 16 + b, 8, stride=2), :] += extra
        for f, at, zone in ((2, 0, 0), (3, 14, 3)):
            for i, extra in enumerate(added(xy, b, f)):
                for n in range(4):
                    turn = (32 * (zone - n)) % 128
                    part = pltpu.roll(extra, turn, 1) if turn else extra
                    moved[pl.ds(i * 512 + n * 128 + at + b, 8, stride=16), :] += jnp.where(lane // 32 == zone, part, 0.0)
    finish(sent_zz)
    for b in range(2):
        for which in range(2):
            for i, extra in enumerate(added(zz, b, 4 + which)):
                tmp[pl.ds((i * 2 + which) * 16 + b, 8, stride=2), :] = extra
    ends = [[tmp[n * 16 + h * 8 : n * 16 + h * 8 + 8, :] for h in range(2)] for n in range(6)]

    def close(ix, carry):
        sums = [jnp.zeros((8, 128), jnp.float32)] * 6
        for step in range(8):
            x = ix * 8 + step
            for i in range(3):
                for h in range(2):
                    low = pltpu.roll(ends[i * 2][h], (128 - x) & 127, 1)
                    high = pltpu.roll(ends[i * 2 + 1][h], (159 - x) & 127, 1)
                    extra = jnp.where((lane & 31) == 0, low, jnp.where((lane & 31) == 31, high, 0.0))
                    fresh = out_ref[i * 32 + x, h * 8 : h * 8 + 8, :] + extra
                    out_ref[i * 32 + x, h * 8 : h * 8 + 8, :] = fresh
                    sums[i * 2 + h] = sums[i * 2 + h] + fresh
        for i in range(3):
            for h in range(2):
                acc[pl.ds(pl.multiple_of((i * 4 + ix) * 16 + h * 8, 8), 8), :] = sums[i * 2 + h]
        return carry

    lax.fori_loop(0, 4, close, 0)

    stores = [pltpu.make_async_copy(out_ref, fresh_hbm, out_sem.at[0])]
    stores[0].start()
    for load in loads[2:]:
        load.wait()
    fold, mean = fold_ref[...].astype(jnp.bfloat16), mean_ref[...].astype(jnp.bfloat16)
    folded = sum(dot(part, fold) for part in thirds(acc[...])) * pick_ref[...]
    rows = sum(dot(mean, part) for part in thirds(folded))
    wide_row, wide_lane = iota((8, 256), 0), iota((8, 256), 1)

    def shrink(level):
        return jnp.where(level == 0, 1.0, jnp.where(level == 1, 0.125, 0.015625))

    rows = rows * jnp.where(wide_row == 0, shrink(level_ref[0]), shrink(level_ref[1]))
    owners = jnp.where(wide_row == 0, owner_ref[0], owner_ref[1]).astype(jnp.float32)
    rows = jnp.where(wide_lane == 192, owners, rows)
    gap = jnp.zeros((2, 128), jnp.float32)
    spot = half * 2 + sub // 2
    mine = pl.ds(pl.multiple_of(spot * 8, 8), 8)
    t1[mine, :] = jnp.concatenate(
        [rows[0:1, 0:128], rows[0:1, 128:256], gap, rows[1:2, 0:128], rows[1:2, 128:256], gap], axis=0)

    def share(ref, targets, first):
        return start([remote(ref, ref, first + n, device) for n, device in enumerate(targets)])

    sent = share(t1.at[mine], [mates[k - 1] for k in (2, 4, 6)], 40)

    on = [jnp.where(slot_ref[0] == b, 10.0, 0.0) for b in range(2)]
    flat_both = both.reshape(2048, 128)

    def penalise(x, carry):
        part = solid[pl.ds(pl.multiple_of(x * 8, 8), 8), :]
        at = (x // 16) * 64 + lax.rem(x, 16)
        for b in range(2):
            flat_both[pl.ds((at + 48) * 16 + b, 8, stride=2), :] = part * on[b]
        for h in range(2):
            rows = slice(h * 8, h * 8 + 8)
            chi = both[at + 48, rows, :]
            scale = 1.0 / (1.0 + chi)
            both[at + 48, rows, :] = scale
            for c in range(3):
                both[at + c * 16, rows, :] = (uv[c * 32 + x, rows, :] + chi * speed_ref[0, c]) * scale
        return carry

    lax.fori_loop(0, 32, penalise, 0)
    stores += start([pltpu.make_async_copy(both, both_hbm, out_sem.at[1])])
    finish(sent)
    first = ring * 8
    at = pl.ds(pl.multiple_of(first, 8), 8)
    for t in range(2):
        g[at, t * 128 : t * 128 + 128] = t1[pl.ds(t, 8, stride=4), :]
    sent = share(g.at[at], on_z, 43)

    theirs = nbr[pl.ds(pl.multiple_of(lax.bitwise_xor(me, 1) * 8, 8), 8), :]
    owners = [jnp.full((8, 128), owner_ref[b], jnp.int32) for b in range(2)]
    owners += [jnp.broadcast_to(theirs[:, 12 + b : 13 + b], (8, 128)) for b in range(2)]
    columns = [owner & 31 for owner in owners]
    bands = [owner // 32 for owner in owners]

    def pick_y(py, carry):
        found = []
        for n in range(2):
            row_of = inv_y[pl.ds(pl.multiple_of(py * 8, 8), 8), n * 128 : n * 128 + 128]
            found += [jnp.where(columns[k] == py, row_of, carry[n * 4 + k]) for k in range(4)]
        return tuple(found)

    for n, part in enumerate(lax.fori_loop(0, 32, pick_y, (zero,) * 8)):
        near_y[pl.ds((n % 4 // 2) * 32 + (n // 4) * 16 + n % 2, 8, stride=2), :] = part

    def pick_xz(px, carry):
        found = []
        for n in range(4):
            row_of = inv_xz[pl.ds(pl.multiple_of((n // 2) * 128 + px * 16 + (n % 2) * 8, 8), 8), :]
            found += [jnp.where(bands[k] == px, row_of, carry[n * 4 + k]) for k in range(4)]
        return tuple(found)

    for n, part in enumerate(lax.fori_loop(0, 8, pick_xz, (zero,) * 16)):
        k, n = n % 4, n // 4
        to = (k // 2) * 64 + (n // 2) * 32 + (k % 2) * 16 + (n % 2) * 8
        chosen[to : to + 8, :] = part
    finish(sent)
    finish(share(g.at[pl.ds(pl.multiple_of(y * 64, 64), 64)], on_y, 50))

    own, other = solve(g[...], fwd_y, fwd_xz, spectral, chosen, near_y)
    mine_s[:, 0:96] = other
    sent = start([remote(mine_s, peer_s, 53, mates[0])])
    finish(sent)
    field[...] = lift(own + peer_s[:, 0:96], match, spread_z)
    stores += start([pltpu.make_async_copy(field, field_hbm, out_sem.at[2])])
    finish(stores)


def halves(table):
    high = table.astype(ml_dtypes.bfloat16).astype(np.float64)
    low = (table - high).astype(ml_dtypes.bfloat16).astype(np.float64)
    return high, low


def solve_tables():
    space = np.arange(128)
    px, ix, iz = space // 16, (space // 4) % 4, space % 4
    x, z = 4 * px + ix, iz
    kx, kz = space // 4, space % 4
    iy, py = space // 32, space % 32
    y = 4 * py + iy
    ky = space
    theta = 2.0 * np.pi * ((kx[:, None] * x[None, :] % 32) / 32.0 + (kz[:, None] * z[None, :] % 4) / 4.0)
    phi = 2.0 * np.pi * ((y[:, None] * ky[None, :]) % 128) / 128.0
    high, low = halves(np.concatenate([np.cos(phi), -np.sin(phi)], axis=1))
    fwd_y = np.concatenate([high, high, low], axis=0)
    high, low = halves(np.concatenate([np.cos(theta), np.sin(theta)], axis=0))
    fwd_xz = np.concatenate([high, low], axis=1)
    inv_xz = np.concatenate([np.cos(theta.T), np.sin(theta.T)], axis=0).astype(np.float32)
    line = np.arange(256)
    turn = 2.0 * np.pi * (((4 * (line // 8) + (line % 8) // 2)[:, None] * ky[None, :]) % 128) / 128.0
    inv_y = (np.concatenate([np.cos(turn), -np.sin(turn)], axis=1) / 16384.0).astype(np.float32)

    def waves(index, length):
        signed = np.where(index < (length + 1) // 2, index, index - length)
        full = signed * (2.0 * math.pi / length)
        return full, np.where(index == length // 2, 0.0, full)

    full_x, slope_x = waves(kx, GX)
    full_y, slope_y = waves(ky, GY)
    full_z, slope_z = waves(kz, GZ)
    square = (full_x**2 + full_z**2)[:, None] + (full_y**2)[None, :]
    inverse = np.where(square > 0, 1.0 / np.where(square > 0, square, 1.0), 0.0)
    spectral = np.concatenate([inverse * slope_x[:, None], inverse * slope_y[None, :], inverse * slope_z[:, None]])
    src = np.arange(96)
    row = np.arange(192)
    src_c, src_b, src_ix, src_iz = src // 32, (src // 16) % 2, (src // 4) % 4, src % 4
    match = ((src_c * 4 + src_ix)[None, :] == (row // 16)[:, None]) & (src_b[None, :] == (row % 2)[:, None])
    spread_z = src_iz[:, None] == ((np.arange(128) % 32) // 8)[None, :]
    return tuple(a.astype(np.float32) for a in (inv_xz, inv_y, fwd_y, fwd_xz, spectral, match * 1.0, spread_z * 1.0))


def cut(array):
    high = array.astype(jnp.bfloat16)
    return high, (array - high.astype(jnp.float32)).astype(jnp.bfloat16)


def thirds(array):
    high = array.astype(jnp.bfloat16)
    rest = array - high.astype(jnp.float32)
    middle = rest.astype(jnp.bfloat16)
    return high, middle, (rest - middle.astype(jnp.float32)).astype(jnp.bfloat16)


def dot(left, right):
    return jnp.dot(left, right, preferred_element_type=jnp.float32)


def dot_nt(left, right):
    return lax.dot_general(left, right, (((1,), (1,)), ((), ())), preferred_element_type=jnp.float32)


def solve(sent, fwd_y, fwd_xz, spectral, chosen, near_y):
    hot = (sent[:, 192:193] == iota((256, 256), 1).astype(jnp.float32)).astype(jnp.bfloat16)
    high, low = cut(sent.T)
    columns = dot(high, hot) + dot(low, hot)
    lane = iota((48, 128), 1)
    rows = []
    for px in range(8):
        held = None
        for iy in range(4):
            part = columns[iy * 48 : iy * 48 + 48, (px // 4) * 128 : (px // 4) * 128 + 128]
            turn = ((iy - px % 4) * 32) % 128
            if turn:
                part = pltpu.roll(part, turn, 1)
            held = part if held is None else jnp.where(lane >= iy * 32, part, held)
        rows.append(held)
    high, low = cut(jnp.concatenate(rows, axis=0))
    table = fwd_y[...].astype(jnp.bfloat16)
    waves_y = dot(jnp.concatenate([high, low], axis=1), table[0:256]) + dot(high, table[256:384])
    stacked = jnp.concatenate(
        [
            jnp.concatenate([waves_y[px * 48 + c * 16 : px * 48 + c * 16 + 16, :] for px in range(8)], axis=0)
            for c in range(3)
        ],
        axis=1,
    )
    high, low = cut(stacked)
    table = fwd_xz[...].astype(jnp.bfloat16)
    full = dot(table, jnp.concatenate([high, high], axis=0)) + dot(table[:, 0:128], low)
    slope_x, slope_y, slope_z = spectral[0:128, :], spectral[128:256, :], spectral[256:384, :]
    real, imag = [], []
    for c in range(3):
        low = full[:, c * 256 : c * 256 + 128]
        high = full[:, c * 256 + 128 : c * 256 + 256]
        real.append(low[0:128] + high[128:256])
        imag.append(high[0:128] - low[128:256])

    def cross(hat):
        return [
            slope_y * hat[2] - slope_z * hat[1],
            slope_z * hat[0] - slope_x * hat[2],
            slope_x * hat[1] - slope_y * hat[0],
        ]

    cross_real, cross_imag = cross(real), cross(imag)
    high, low = cut(jnp.concatenate([part for c in range(3) for part in (-cross_imag[c], cross_real[c])], axis=1))
    chosen_high, chosen_low = cut(chosen[...])
    near = dot(jnp.concatenate([chosen_high, chosen_low], axis=1), jnp.concatenate([high, high], axis=0))
    near = near + dot(chosen_high, low)
    shares = []
    for side in range(2):
        lines = []
        for c in range(3):
            low = near[side * 64 : side * 64 + 64, c * 256 : c * 256 + 128]
            high = near[side * 64 : side * 64 + 64, c * 256 + 128 : c * 256 + 256]
            lines.append(jnp.concatenate([low[0:32] - high[32:64], high[0:32] + low[32:64]], axis=1))
        high, low = cut(jnp.concatenate(lines, axis=0))
        near_high, near_low = cut(jnp.concatenate([near_y[side * 32 + n * 16 : side * 32 + n * 16 + 16, :] for n in range(2)], axis=1))
        shares.append(dot_nt(near_high, high) + (dot_nt(near_high, low) + dot_nt(near_low, high)))
    return shares


def lift(share, match, spread_z):
    high, low = cut(jnp.concatenate([share] * 12, axis=0) * match[...])
    table = spread_z[...].astype(jnp.bfloat16)
    return dot(high, table) + dot(low, table)


def final_kernel(both_hbm, field_hbm, fresh_hbm, fresh_out, out_hbm, both, field, fresh, moved, sem, out_sem):
    halves_of = [pl.ds(n * 64, 64) for n in range(2)]
    loads = [pltpu.make_async_copy(field_hbm, field, sem.at[0])]
    loads += [pltpu.make_async_copy(both_hbm.at[part], both.at[part], sem.at[1 + n]) for n, part in enumerate(halves_of)]
    loads += [pltpu.make_async_copy(fresh_hbm, fresh, sem.at[3])]
    for load in loads:
        load.start()
    loads[0].wait()
    stores = []
    for n in range(2):
        loads[1 + n].wait()
        for ix in (n * 2, n * 2 + 1):
            lifted = [[field[(c * 4 + ix) * 16 + h * 8 : (c * 4 + ix) * 16 + h * 8 + 8, :] for h in range(2)] for c in range(3)]
            for x in range(ix * 8, ix * 8 + 8):
                at = n * 64 + x % 16
                for h in range(2):
                    rows = slice(h * 8, h * 8 + 8)
                    scale = both[at + 48, rows, :]
                    for c in range(3):
                        moved[c, x, rows, :] = both[at + c * 16, rows, :] + lifted[c][h] * scale
        planes = pl.ds(n * 16, 16)
        stores.append(pltpu.make_async_copy(moved.at[:, planes], out_hbm.at[:, planes], out_sem.at[n]))
        stores[-1].start()
    loads[3].wait()
    stores.append(pltpu.make_async_copy(fresh, fresh_out, out_sem.at[2]))
    stores[-1].start()
    for copy in stores:
        copy.wait()


SMEM = pl.BlockSpec(memory_space=pltpu.SMEM)
ANY = pl.BlockSpec(memory_space=pl.ANY)
LIMIT = 62 * 2**20


def f32(*shape):
    return jax.ShapeDtypeStruct(shape, jnp.float32)


def scratch(*shape):
    return pltpu.VMEM(shape, jnp.float32)


def split(array):
    return array.reshape(2, 3, 256, 128).transpose(1, 2, 0, 3)


def join(array):
    return array.reshape(3, 256, 2, 128).transpose(2, 0, 1, 3).reshape(2, 3, 32768)


def body(vorticity, velocity, level_map, patch_owner, neighbours, fish_slot, fish_mask, fish_speed):
    w, u = split(vorticity), split(velocity)
    w, u = w.reshape(96, 16, 128), u.reshape(96, 16, 128)
    field = f32(96, 16, 128)

    def faces(count):
        return [scratch(rows * count, 128) for rows in (96, 192, 96, 96)]

    sources = (w, u, fish_mask.reshape(256, 128), *(jnp.asarray(a) for a in fold_tables() + solve_tables()))
    fresh, both, lifted = pl.pallas_call(
        front_kernel,
        out_shape=(field, f32(128, 16, 128), f32(192, 128)),
        in_specs=[SMEM] * 4 + [ANY] * 14,
        out_specs=(ANY,) * 3,
        scratch_shapes=[
            *(scratch(*array.shape) for array in sources),
            scratch(96, 16, 128),
            scratch(128, 16, 128),
            scratch(192, 128),
            *faces(4),
            *faces(2),
            scratch(192, 128),
            pltpu.VMEM((8, 128), jnp.int32),
            pltpu.VMEM((64, 128), jnp.int32),
            scratch(192, 128),
            scratch(32, 128),
            scratch(256, 256),
            scratch(128, 128),
            scratch(64, 128),
            scratch(16, 128),
            scratch(16, 128),
            pltpu.SMEM((1,), jnp.int32),
            pltpu.SemaphoreType.DMA((14,)),
            pltpu.SemaphoreType.DMA((3,)),
            pltpu.SemaphoreType.DMA((56,)),
            pltpu.SemaphoreType.DMA((56,)),
        ],
        compiler_params=pltpu.CompilerParams(collective_id=0, has_side_effects=True, vmem_limit_bytes=LIMIT),
        name="front",
    )(neighbours, level_map, patch_owner, fish_speed, fish_slot, *sources)
    fresh, moved = pl.pallas_call(
        final_kernel,
        out_shape=(field, f32(3, 32, 16, 128)),
        in_specs=[ANY] * 3,
        out_specs=(ANY, ANY),
        scratch_shapes=[
            scratch(128, 16, 128),
            scratch(192, 128),
            scratch(96, 16, 128),
            scratch(3, 32, 16, 128),
            pltpu.SemaphoreType.DMA((4,)),
            pltpu.SemaphoreType.DMA((3,)),
        ],
        compiler_params=pltpu.CompilerParams(vmem_limit_bytes=LIMIT),
        name="final",
    )(both, lifted, fresh)
    return join(fresh), join(moved)


def solution(mesh):
    blocks = ("blk", "sub")
    placed = (
        P(blocks, None, None),
        P(blocks, None, None),
        P(blocks),
        P(blocks),
        P(blocks, None),
        P(blocks),
        P(blocks, None),
        P(blocks, None),
    )
    return jax.shard_map(
        body,
        mesh=mesh,
        in_specs=placed,
        out_specs=(P(blocks, None, None), P(blocks, None, None)),
        check_vma=False,
    )
```

```python
import math

import jax
import jax.numpy as jnp
import ml_dtypes
import numpy as np
from jax import lax
from jax.experimental import pallas as pl
from jax.experimental.pallas import tpu as pltpu
from jax.sharding import PartitionSpec as P

MESH = pl.DeviceIdType.MESH
RINGS = 32
MATES = (2, 3, 4, 5, 6, 7, 1)
STEPS_Z = (4, 3, 5, 2, 6, 1, 7)
STEPS_Y = (2, 1, 3)
GX = 32
GY = 128
GZ = 4


def fold_tables():
    row = np.arange(192)
    lane = np.arange(128)
    n = np.arange(256)
    row_c_ix, row_iy, row_b = row // 16, (row % 16) // 4, row % 2
    lane_iz = (lane % 32) // 8
    live = n < 192
    fold = ((lane_iz[:, None] == n[None, :] % 4) & live[None, :]) * 1.0
    pick = ((n[None, :] // 4 == (row_iy * 12 + row_c_ix)[:, None]) & live[None, :]) * 1.0
    mean = (np.arange(8)[:, None] == row_b[None, :]) / 512.0
    return fold.astype(np.float32), pick.astype(np.float32), mean.astype(np.float32)


def iota(shape, dim):
    return lax.broadcasted_iota(jnp.int32, shape, dim)


def place():
    blk, sub = lax.axis_index("blk"), lax.axis_index("sub")
    return blk // 2, lax.rem(blk, 2), sub


def row_pair(first, second):
    return jnp.where((iota((8, 128), 0) & 1) == 0, first, second)


class Chunk:
    def __init__(self, first, count, s1, r1, s2, r2, sem):
        self.first, self.count = first, count
        self.s1, self.r1, self.s2, self.r2, self.sem = s1, r1, s2, r2, sem
        self.rows = 12 * count

    def at(self, b, f, c):
        return (b * self.count + f - self.first) * 6 + c

    def put(self, b, f, c, plane):
        self.s1[pl.ds(self.at(b, f, c), 8, stride=self.rows), :] = plane

    def own(self, b, f, c):
        return self.s1[pl.ds(self.at(b, f, c), 8, stride=self.rows), :]

    def ghost(self, b, f, c):
        return self.r2[pl.ds(self.at(b, f, c), 8, stride=self.rows), :]

    def piece(self, which, count=1):
        return pl.ds(pl.multiple_of(which * self.rows, 8), count * self.rows)


def front_kernel(nb_ref, level_ref, owner_ref, speed_ref, slot_hbm, *refs):
    sources, (fresh_hbm, both_hbm, share_hbm), refs = refs[:11], refs[11:14], refs[14:]
    held, refs = refs[:11], refs[11:]
    wv, uv, solid, fold_ref, pick_ref, mean_ref, inv_xz, inv_y, fwd_y, fwd_xz, spectral = held
    (out_ref, both, s1a, r1a, s2a, r2a, s1b, r1b, s2b, r2b, tmp, nbs, nbr, acc, t1, g, chosen, near_y, mine_s, peer_s, share_s,
     slot_ref, in_sem, out_sem, ssem, rsem) = refs
    ring, half, sub = place()
    me = half * 4 + sub
    y, z = ring // 8, lax.rem(ring, 8)
    loads = [pltpu.make_async_copy(src, dst, in_sem.at[n]) for n, (src, dst) in enumerate(zip(sources, held))]
    loads.append(pltpu.make_async_copy(slot_hbm, slot_ref, in_sem.at[11]))
    for load in loads:
        load.start()

    def mate(k):
        other = lax.bitwise_xor(me, k)
        return (ring * 2 + other // 4, lax.rem(other, 4))

    def beside(step):
        return (lax.rem(ring + step + RINGS, RINGS) * 2 + half, sub)

    def along_z(k):
        return ((y * 8 + lax.rem(z + k, 8)) * 2 + half, sub)

    def along_y(k):
        return ((lax.rem(y + k, 4) * 8 + z) * 2 + half, sub)

    mates = [mate(k) for k in MATES]
    on_z = [along_z(k) for k in STEPS_Z]
    on_y = [along_y(k) for k in STEPS_Y]
    everyone = mates + [beside(1), beside(-1)] + on_z + on_y
    barrier = pltpu.get_barrier_semaphore()
    for device in everyone:
        pl.semaphore_signal(barrier, inc=1, device_id=device, device_id_type=MESH)

    lane = iota((8, 128), 1)
    row = iota((8, 128), 0)
    wants = jnp.zeros((8, 128), jnp.int32)
    for b in range(2):
        for f in range(6):
            wants = jnp.where(lane == b * 6 + f, nb_ref[b, f] + half * 8, wants)
        wants = jnp.where(lane == 12 + b, owner_ref[b], wants)
    nbs[...] = wants
    nbr[pl.ds(pl.multiple_of(me * 8, 8), 8), :] = wants
    for load in loads[:2]:
        load.wait()

    flat = (wv.reshape(1536, 128), uv.reshape(1536, 128))

    def source(c):
        return flat[c // 3], (c % 3) * 512

    def remote(src, dst, sem, device):
        return pltpu.make_async_remote_copy(
            src_ref=src, dst_ref=dst, send_sem=ssem.at[sem], recv_sem=rsem.at[sem],
            device_id=device, device_id_type=MESH)

    def start(copies):
        for copy in copies:
            copy.start()
        return copies

    def finish(copies):
        for copy in copies:
            copy.wait()

    xy = Chunk(0, 4, s1a, r1a, s2a, r2a, 8)
    zz = Chunk(4, 2, s1b, r1b, s2b, r2b, 24)

    def scatter_faces(part):
        copies = start([
            remote(part.s1.at[part.piece(lax.bitwise_xor(me, k))], part.r1.at[part.piece(4 + me)], part.sem + k - 1, mate(k))
            for k in MATES
        ])
        part.r1[part.piece(4 + me), :] = part.s1[part.piece(me), :]
        return copies

    def forward_faces(part):
        return start([
            remote(part.r1.at[part.piece(8, 4)], part.r1.at[part.piece(0, 4)], part.sem + 7, beside(1)),
            remote(part.r1.at[part.piece(4, 4)], part.r1.at[part.piece(12, 4)], part.sem + 8, beside(-1)),
        ])

    def return_faces(part):
        copies = start([
            remote(part.s2.at[part.piece(lax.bitwise_xor(me, k))], part.r2.at[part.piece(me)], part.sem + 8 + k, mate(k))
            for k in MATES
        ])
        part.r2[part.piece(me), :] = part.s2[part.piece(me), :]
        return copies

    for c in range(6):
        ref, base = source(c)
        for b in range(2):
            for f, x in ((0, 0), (1, 31)):
                xy.put(b, f, c, ref[pl.ds(base + x * 16 + b, 8, stride=2), :])
            low = high = jnp.zeros((8, 128), jnp.float32)
            for n in range(4):
                first = ref[pl.ds(base + n * 128 + b, 8, stride=16), :]
                last = ref[pl.ds(base + n * 128 + 14 + b, 8, stride=16), :]
                if n:
                    first = pltpu.roll(first, 32 * n, 1)
                if n != 3:
                    last = pltpu.roll(last, (32 * n + 32) % 128, 1)
                here = lane // 32 == n
                low = jnp.where(here, first, low)
                high = jnp.where(here, last, high)
            xy.put(b, 2, c, low)
            xy.put(b, 3, c, high)

    pl.semaphore_wait(barrier, len(everyone))
    mine = pl.ds(pl.multiple_of(me * 8, 8), 8)
    sent_wants = start([remote(nbs, nbr.at[mine], k - 1, mate(k)) for k in MATES])
    sent_xy = scatter_faces(xy)

    def gather_z(x, held):
        at_low = (lane & 31) == x
        at_high = (lane & 31) == ((x + 31) & 31)
        fresh = []
        for c in range(6):
            ref, base = source(c)
            for h in range(2):
                plane = ref[pl.ds(pl.multiple_of(base + x * 16 + h * 8, 8), 8), :]
                turned = pltpu.roll(plane, x, 1)
                low, high = held[(c * 2 + h) * 2], held[(c * 2 + h) * 2 + 1]
                fresh += [jnp.where(at_low, turned, low), jnp.where(at_high, turned, high)]
        return tuple(fresh)

    zero = jnp.zeros((8, 128), jnp.float32)
    packed = lax.fori_loop(0, 32, gather_z, (zero,) * 24)
    for c in range(6):
        for which in range(2):
            for h in range(2):
                at = (c * 2 + which) * 16 + h * 8
                plane = packed[(c * 2 + h) * 2 + which]
                tmp[at : at + 8, :] = pltpu.roll(plane, 97, 1) if which else plane
    for c in range(6):
        for which in range(2):
            for b in range(2):
                zz.put(b, 4 + which, c, tmp[pl.ds((c * 2 + which) * 16 + b, 8, stride=2), :])
    sent_zz = scatter_faces(zz)

    def scale(level):
        return lax.shift_left(1, level).astype(jnp.float32)

    sizes = [scale(level_ref[b]) for b in range(2)]
    slopes_of = [0.05 * 0.5 * size for size in sizes]
    spread_of = [0.05 * 0.1 * (size * size) for size in sizes]
    slope = row_pair(*slopes_of)
    spread = row_pair(*spread_of)

    def around(x, c, h):
        ref = (wv, uv)[c // 3]
        at = (c % 3) * 32 + x
        rows = slice(h * 8, h * 8 + 8)
        here = ref[at, rows, :]
        left = jnp.zeros_like(here) if isinstance(x, int) and x == 0 else ref[at - 1, rows, :]
        right = jnp.zeros_like(here) if isinstance(x, int) and x == 31 else ref[at + 1, rows, :]
        if h == 0:
            before = jnp.where(row < 2, 0.0, pltpu.roll(here, 2, 0))
            after = ref[at, 2:10, :]
        else:
            before = ref[at, 6:14, :]
            after = jnp.where(row >= 6, 0.0, pltpu.roll(here, 6, 0))
        before = pltpu.roll(jnp.where(lane >= 96, before, here), 32, 1)
        after = pltpu.roll(jnp.where(lane < 32, after, here), 96, 1)
        below = jnp.where((lane & 31) == 0, 0.0, pltpu.roll(here, 1, 1))
        above = jnp.where((lane & 31) == 31, 0.0, pltpu.roll(here, 127, 1))
        return here, (left, right), (before, after), (below, above)

    def plane(x):
        for h in range(2):
            parts = [around(x, c, h) for c in range(6)]
            heres = [part[0] for part in parts]
            slopes = [[part[1 + d][1] - part[1 + d][0] for d in range(3)] for part in parts]
            for i in range(3):
                turn = heres[0] * slopes[3 + i][0] + heres[1] * slopes[3 + i][1] + heres[2] * slopes[3 + i][2]
                turn -= heres[3] * slopes[i][0] + heres[4] * slopes[i][1] + heres[5] * slopes[i][2]
                ends = [part for d in range(3) for part in parts[i][1 + d]]
                total = (ends[0] + ends[1]) + (ends[2] + ends[3]) + (ends[4] + ends[5])
                out_ref[i * 32 + x, h * 8 : h * 8 + 8, :] = (
                    heres[i] + slope * turn + spread * (total - 6.0 * heres[i])
                )

    def planes(low, high):
        def step(x, carry):
            plane(x)
            return carry

        lax.fori_loop(low, high, step, 0)

    plane(0)
    planes(1, 15)
    finish(sent_wants)
    finish(sent_xy)
    sent_xy = forward_faces(xy)
    planes(15, 23)
    finish(sent_zz)
    sent_zz = forward_faces(zz)
    planes(23, 31)
    plane(31)

    slot = iota((8, 32), 1)
    dead_low = (ring == 0).astype(jnp.int32)
    dead_high = (ring == RINGS - 1).astype(jnp.int32)
    alive = 1 - dead_low * (slot < 8).astype(jnp.int32) - dead_high * (slot >= 24).astype(jnp.int32)
    alive = alive.astype(jnp.float32)

    def select(part):
        wanted = nbr[pl.ds(0, 8, stride=8), :]
        for f in range(part.first, part.first + part.count):
            hot = jnp.concatenate(
                [jnp.where(wanted[:, b * 6 + f : b * 6 + f + 1] == slot, alive, 0.0) for b in range(2)], axis=0)
            data = jnp.concatenate(
                [part.r1[pl.ds(part.at(0, f ^ 1, c), 32, stride=6 * part.count), :] for c in range(6)], axis=1)
            hot = hot.astype(jnp.bfloat16)
            got = sum(dot(hot, third) for third in thirds(data))
            for b in range(2):
                for c in range(6):
                    part.s2[pl.ds(part.at(b, f, c), 8, stride=part.rows), :] = (
                        got[b * 8 : b * 8 + 8, c * 128 : c * 128 + 128]
                    )

    finish(sent_xy)
    select(xy)
    sent_xy = return_faces(xy)
    finish(sent_zz)
    select(zz)
    sent_zz = return_faces(zz)

    moved = out_ref.reshape(1536, 128)

    def added(part, b, f):
        ghosts = [part.ghost(b, f, c) for c in range(6)]
        vort, veloc = part.own(b, f, f // 2), part.own(b, f, 3 + f // 2)
        sign = slopes_of[b] * (1.0 if f % 2 else -1.0)
        vort, veloc = vort * sign, spread_of[b] - veloc * sign
        return [vort * ghosts[3 + i] + veloc * ghosts[i] for i in range(3)]

    finish(sent_xy)
    for b in range(2):
        for f, x in ((0, 0), (1, 31)):
            for i, extra in enumerate(added(xy, b, f)):
                moved[pl.ds(i * 512 + x * 16 + b, 8, stride=2), :] += extra
        for f, at, zone in ((2, 0, 0), (3, 14, 3)):
            for i, extra in enumerate(added(xy, b, f)):
                for n in range(4):
                    turn = (32 * (zone - n)) % 128
                    part = pltpu.roll(extra, turn, 1) if turn else extra
                    moved[pl.ds(i * 512 + n * 128 + at + b, 8, stride=16), :] += jnp.where(lane // 32 == zone, part, 0.0)
    finish(sent_zz)
    for b in range(2):
        for which in range(2):
            for i, extra in enumerate(added(zz, b, 4 + which)):
                tmp[pl.ds((i * 2 + which) * 16 + b, 8, stride=2), :] = extra
    ends = [[tmp[n * 16 + h * 8 : n * 16 + h * 8 + 8, :] for h in range(2)] for n in range(6)]

    def close(ix, carry):
        sums = [jnp.zeros((8, 128), jnp.float32)] * 6
        for step in range(8):
            x = ix * 8 + step
            for i in range(3):
                for h in range(2):
                    low = pltpu.roll(ends[i * 2][h], (128 - x) & 127, 1)
                    high = pltpu.roll(ends[i * 2 + 1][h], (159 - x) & 127, 1)
                    extra = jnp.where((lane & 31) == 0, low, jnp.where((lane & 31) == 31, high, 0.0))
                    fresh = out_ref[i * 32 + x, h * 8 : h * 8 + 8, :] + extra
                    out_ref[i * 32 + x, h * 8 : h * 8 + 8, :] = fresh
                    sums[i * 2 + h] = sums[i * 2 + h] + fresh
        for i in range(3):
            for h in range(2):
                acc[pl.ds(pl.multiple_of((i * 4 + ix) * 16 + h * 8, 8), 8), :] = sums[i * 2 + h]
        return carry

    lax.fori_loop(0, 4, close, 0)

    stores = [pltpu.make_async_copy(out_ref, fresh_hbm, out_sem.at[0])]
    stores[0].start()
    for load in loads[2:]:
        load.wait()
    fold, mean = fold_ref[...].astype(jnp.bfloat16), mean_ref[...].astype(jnp.bfloat16)
    folded = sum(dot(part, fold) for part in thirds(acc[...])) * pick_ref[...]
    rows = sum(dot(mean, part) for part in thirds(folded))
    wide_row, wide_lane = iota((8, 256), 0), iota((8, 256), 1)

    def shrink(level):
        return jnp.where(level == 0, 1.0, jnp.where(level == 1, 0.125, 0.015625))

    rows = rows * jnp.where(wide_row == 0, shrink(level_ref[0]), shrink(level_ref[1]))
    owners = jnp.where(wide_row == 0, owner_ref[0], owner_ref[1]).astype(jnp.float32)
    rows = jnp.where(wide_lane == 192, owners, rows)
    gap = jnp.zeros((2, 128), jnp.float32)
    spot = half * 2 + sub // 2
    mine = pl.ds(pl.multiple_of(spot * 8, 8), 8)
    t1[mine, :] = jnp.concatenate(
        [rows[0:1, 0:128], rows[0:1, 128:256], gap, rows[1:2, 0:128], rows[1:2, 128:256], gap], axis=0)

    def share(ref, targets, first):
        return start([remote(ref, ref, first + n, device) for n, device in enumerate(targets)])

    sent = share(t1.at[mine], [mate(k) for k in (2, 4, 6)], 40)

    on = [jnp.where(slot_ref[0] == b, 10.0, 0.0) for b in range(2)]
    flat_both = both.reshape(2048, 128)

    def penalise(x, carry):
        part = solid[pl.ds(pl.multiple_of(x * 8, 8), 8), :]
        at = (x // 16) * 64 + lax.rem(x, 16)
        for b in range(2):
            flat_both[pl.ds((at + 48) * 16 + b, 8, stride=2), :] = part * on[b]
        for h in range(2):
            rows = slice(h * 8, h * 8 + 8)
            chi = both[at + 48, rows, :]
            scale = 1.0 / (1.0 + chi)
            both[at + 48, rows, :] = scale
            for c in range(3):
                both[at + c * 16, rows, :] = (uv[c * 32 + x, rows, :] + chi * speed_ref[0, c]) * scale
        return carry

    lax.fori_loop(0, 32, penalise, 0)
    stores += start([pltpu.make_async_copy(both, both_hbm, out_sem.at[1])])
    finish(sent)
    first = ring * 8
    at = pl.ds(pl.multiple_of(first, 8), 8)
    for t in range(2):
        g[at, t * 128 : t * 128 + 128] = t1[pl.ds(t, 8, stride=4), :]
    sent = share(g.at[at], on_z, 43)

    theirs = nbr[pl.ds(pl.multiple_of(lax.bitwise_xor(me, 1) * 8, 8), 8), :]
    owners = [jnp.full((8, 128), owner_ref[b], jnp.int32) for b in range(2)]
    owners += [jnp.broadcast_to(theirs[:, 12 + b : 13 + b], (8, 128)) for b in range(2)]
    columns = [owner & 31 for owner in owners]
    bands = [owner // 32 for owner in owners]

    def pick_y(py, carry):
        found = []
        for n in range(2):
            row_of = inv_y[pl.ds(pl.multiple_of(py * 8, 8), 8), n * 128 : n * 128 + 128]
            found += [jnp.where(columns[k] == py, row_of, carry[n * 4 + k]) for k in range(4)]
        return tuple(found)

    for n, part in enumerate(lax.fori_loop(0, 32, pick_y, (zero,) * 8)):
        near_y[pl.ds((n % 4 // 2) * 32 + (n // 4) * 16 + n % 2, 8, stride=2), :] = part

    def pick_xz(px, carry):
        found = []
        for n in range(4):
            row_of = inv_xz[pl.ds(pl.multiple_of((n // 2) * 128 + px * 16 + (n % 2) * 8, 8), 8), :]
            found += [jnp.where(bands[k] == px, row_of, carry[n * 4 + k]) for k in range(4)]
        return tuple(found)

    for n, part in enumerate(lax.fori_loop(0, 8, pick_xz, (zero,) * 16)):
        k, n = n % 4, n // 4
        to = (k // 2) * 64 + (n // 2) * 32 + (k % 2) * 16 + (n % 2) * 8
        chosen[to : to + 8, :] = part
    finish(sent)
    finish(share(g.at[pl.ds(pl.multiple_of(y * 64, 64), 64)], on_y, 50))

    own, other = solve(g[...], fwd_y, fwd_xz, spectral, chosen, near_y)
    mine_s[:, 0:96] = other
    sent = start([remote(mine_s, peer_s, 53, mate(1))])
    finish(sent)
    share_s[:, 0:96] = own + peer_s[:, 0:96]
    stores += start([pltpu.make_async_copy(share_s, share_hbm, out_sem.at[2])])
    finish(stores)


def halves(table):
    high = table.astype(ml_dtypes.bfloat16).astype(np.float64)
    low = (table - high).astype(ml_dtypes.bfloat16).astype(np.float64)
    return high, low


def solve_tables():
    space = np.arange(128)
    px, ix, iz = space // 16, (space // 4) % 4, space % 4
    x, z = 4 * px + ix, iz
    kx, kz = space // 4, space % 4
    iy, py = space // 32, space % 32
    y = 4 * py + iy
    ky = space
    theta = 2.0 * np.pi * ((kx[:, None] * x[None, :] % 32) / 32.0 + (kz[:, None] * z[None, :] % 4) / 4.0)
    phi = 2.0 * np.pi * ((y[:, None] * ky[None, :]) % 128) / 128.0
    high, low = halves(np.concatenate([np.cos(phi), -np.sin(phi)], axis=1))
    fwd_y = np.concatenate([high, high, low], axis=0)
    high, low = halves(np.concatenate([np.cos(theta), np.sin(theta)], axis=0))
    fwd_xz = np.concatenate([high, low], axis=1)
    inv_xz = np.concatenate([np.cos(theta.T), np.sin(theta.T)], axis=0).astype(np.float32)
    line = np.arange(256)
    turn = 2.0 * np.pi * (((4 * (line // 8) + (line % 8) // 2)[:, None] * ky[None, :]) % 128) / 128.0
    inv_y = (np.concatenate([np.cos(turn), -np.sin(turn)], axis=1) / 16384.0).astype(np.float32)

    def waves(index, length):
        signed = np.where(index < (length + 1) // 2, index, index - length)
        full = signed * (2.0 * math.pi / length)
        return full, np.where(index == length // 2, 0.0, full)

    full_x, slope_x = waves(kx, GX)
    full_y, slope_y = waves(ky, GY)
    full_z, slope_z = waves(kz, GZ)
    square = (full_x**2 + full_z**2)[:, None] + (full_y**2)[None, :]
    inverse = np.where(square > 0, 1.0 / np.where(square > 0, square, 1.0), 0.0)
    spectral = np.concatenate([inverse * slope_x[:, None], inverse * slope_y[None, :], inverse * slope_z[:, None]])
    src = np.arange(96)
    row = np.arange(192)
    src_c, src_b, src_ix, src_iz = src // 32, (src // 16) % 2, (src // 4) % 4, src % 4
    match = ((src_c * 4 + src_ix)[None, :] == (row // 16)[:, None]) & (src_b[None, :] == (row % 2)[:, None])
    spread_z = src_iz[:, None] == ((np.arange(128) % 32) // 8)[None, :]
    return tuple(a.astype(np.float32) for a in (inv_xz, inv_y, fwd_y, fwd_xz, spectral, match * 1.0, spread_z * 1.0))


def cut(array):
    high = array.astype(jnp.bfloat16)
    return high, (array - high.astype(jnp.float32)).astype(jnp.bfloat16)


def thirds(array):
    high = array.astype(jnp.bfloat16)
    rest = array - high.astype(jnp.float32)
    middle = rest.astype(jnp.bfloat16)
    return high, middle, (rest - middle.astype(jnp.float32)).astype(jnp.bfloat16)


def dot(left, right):
    return jnp.dot(left, right, preferred_element_type=jnp.float32)


def dot_nt(left, right):
    return lax.dot_general(left, right, (((1,), (1,)), ((), ())), preferred_element_type=jnp.float32)


def solve(sent, fwd_y, fwd_xz, spectral, chosen, near_y):
    hot = (sent[:, 192:193] == iota((256, 256), 1).astype(jnp.float32)).astype(jnp.bfloat16)
    high, low = cut(sent.T)
    columns = dot(high, hot) + dot(low, hot)
    lane = iota((48, 128), 1)
    rows = []
    for px in range(8):
        held = None
        for iy in range(4):
            part = columns[iy * 48 : iy * 48 + 48, (px // 4) * 128 : (px // 4) * 128 + 128]
            turn = ((iy - px % 4) * 32) % 128
            if turn:
                part = pltpu.roll(part, turn, 1)
            held = part if held is None else jnp.where(lane >= iy * 32, part, held)
        rows.append(held)
    high, low = cut(jnp.concatenate(rows, axis=0))
    table = fwd_y[...].astype(jnp.bfloat16)
    waves_y = dot(jnp.concatenate([high, low], axis=1), table[0:256]) + dot(high, table[256:384])
    stacked = jnp.concatenate(
        [
            jnp.concatenate([waves_y[px * 48 + c * 16 : px * 48 + c * 16 + 16, :] for px in range(8)], axis=0)
            for c in range(3)
        ],
        axis=1,
    )
    high, low = cut(stacked)
    table = fwd_xz[...].astype(jnp.bfloat16)
    full = dot(table, jnp.concatenate([high, high], axis=0)) + dot(table[:, 0:128], low)
    slope_x, slope_y, slope_z = spectral[0:128, :], spectral[128:256, :], spectral[256:384, :]
    real, imag = [], []
    for c in range(3):
        low = full[:, c * 256 : c * 256 + 128]
        high = full[:, c * 256 + 128 : c * 256 + 256]
        real.append(low[0:128] + high[128:256])
        imag.append(high[0:128] - low[128:256])

    def cross(hat):
        return [
            slope_y * hat[2] - slope_z * hat[1],
            slope_z * hat[0] - slope_x * hat[2],
            slope_x * hat[1] - slope_y * hat[0],
        ]

    cross_real, cross_imag = cross(real), cross(imag)
    high, low = cut(jnp.concatenate([part for c in range(3) for part in (-cross_imag[c], cross_real[c])], axis=1))
    chosen_high, chosen_low = cut(chosen[...])
    near = dot(jnp.concatenate([chosen_high, chosen_low], axis=1), jnp.concatenate([high, high], axis=0))
    near = near + dot(chosen_high, low)
    shares = []
    for side in range(2):
        lines = []
        for c in range(3):
            low = near[side * 64 : side * 64 + 64, c * 256 : c * 256 + 128]
            high = near[side * 64 : side * 64 + 64, c * 256 + 128 : c * 256 + 256]
            lines.append(jnp.concatenate([low[0:32] - high[32:64], high[0:32] + low[32:64]], axis=1))
        high, low = cut(jnp.concatenate(lines, axis=0))
        near_high, near_low = cut(jnp.concatenate([near_y[side * 32 + n * 16 : side * 32 + n * 16 + 16, :] for n in range(2)], axis=1))
        shares.append(dot_nt(near_high, high) + (dot_nt(near_high, low) + dot_nt(near_low, high)))
    return shares


def lift(share, match, spread_z):
    high, low = cut(jnp.concatenate([share] * 12, axis=0) * match[...])
    table = spread_z[...].astype(jnp.bfloat16)
    return dot(high, table) + dot(low, table)


def final_kernel(both_hbm, share_hbm, fresh_hbm, match_hbm, spread_hbm, fresh_out, out_hbm,
                 both, share, fresh, match, spread_z, field, moved, sem, out_sem):
    halves_of = [pl.ds(n * 64, 64) for n in range(2)]
    loads = [pltpu.make_async_copy(share_hbm, share, sem.at[0])]
    loads += [pltpu.make_async_copy(both_hbm.at[part], both.at[part], sem.at[1 + n]) for n, part in enumerate(halves_of)]
    loads += [pltpu.make_async_copy(fresh_hbm, fresh, sem.at[3])]
    tables = [pltpu.make_async_copy(match_hbm, match, sem.at[4]), pltpu.make_async_copy(spread_hbm, spread_z, sem.at[5])]
    for load in loads[:1] + tables + loads[1:]:
        load.start()
    for load in loads[:1] + tables:
        load.wait()
    field[...] = lift(share[:, 0:96], match, spread_z)
    stores = []
    for n in range(2):
        loads[1 + n].wait()
        for ix in (n * 2, n * 2 + 1):
            lifted = [[field[(c * 4 + ix) * 16 + h * 8 : (c * 4 + ix) * 16 + h * 8 + 8, :] for h in range(2)] for c in range(3)]
            for x in range(ix * 8, ix * 8 + 8):
                at = n * 64 + x % 16
                for h in range(2):
                    rows = slice(h * 8, h * 8 + 8)
                    scale = both[at + 48, rows, :]
                    for c in range(3):
                        moved[c, x, rows, :] = both[at + c * 16, rows, :] + lifted[c][h] * scale
        planes = pl.ds(n * 16, 16)
        stores.append(pltpu.make_async_copy(moved.at[:, planes], out_hbm.at[:, planes], out_sem.at[n]))
        stores[-1].start()
    loads[3].wait()
    stores.append(pltpu.make_async_copy(fresh, fresh_out, out_sem.at[2]))
    stores[-1].start()
    for copy in stores:
        copy.wait()


SMEM = pl.BlockSpec(memory_space=pltpu.SMEM)
ANY = pl.BlockSpec(memory_space=pl.ANY)
LIMIT = 62 * 2**20


def f32(*shape):
    return jax.ShapeDtypeStruct(shape, jnp.float32)


def scratch(*shape):
    return pltpu.VMEM(shape, jnp.float32)


def split(array):
    return array.reshape(2, 3, 256, 128).transpose(1, 2, 0, 3)


def join(array):
    return array.reshape(3, 256, 2, 128).transpose(2, 0, 1, 3).reshape(2, 3, 32768)


def body(vorticity, velocity, level_map, patch_owner, neighbours, fish_slot, fish_mask, fish_speed):
    w, u = split(vorticity), split(velocity)
    w, u = w.reshape(96, 16, 128), u.reshape(96, 16, 128)
    field = f32(96, 16, 128)

    def faces(count):
        return [scratch(rows * count, 128) for rows in (96, 192, 96, 96)]

    *tables, match, spread_z = (jnp.asarray(a) for a in fold_tables() + solve_tables())
    sources = (w, u, fish_mask.reshape(256, 128), *tables)
    fresh, both, share = pl.pallas_call(
        front_kernel,
        out_shape=(field, f32(128, 16, 128), f32(16, 128)),
        in_specs=[SMEM] * 4 + [ANY] * 12,
        out_specs=(ANY,) * 3,
        scratch_shapes=[
            *(scratch(*array.shape) for array in sources),
            scratch(96, 16, 128),
            scratch(128, 16, 128),
            *faces(4),
            *faces(2),
            scratch(192, 128),
            pltpu.VMEM((8, 128), jnp.int32),
            pltpu.VMEM((64, 128), jnp.int32),
            scratch(192, 128),
            scratch(32, 128),
            scratch(256, 256),
            scratch(128, 128),
            scratch(64, 128),
            scratch(16, 128),
            scratch(16, 128),
            scratch(16, 128),
            pltpu.SMEM((1,), jnp.int32),
            pltpu.SemaphoreType.DMA((12,)),
            pltpu.SemaphoreType.DMA((3,)),
            pltpu.SemaphoreType.DMA((56,)),
            pltpu.SemaphoreType.DMA((56,)),
        ],
        compiler_params=pltpu.CompilerParams(collective_id=0, has_side_effects=True, vmem_limit_bytes=LIMIT),
        name="front",
    )(neighbours, level_map, patch_owner, fish_speed, fish_slot, *sources)
    fresh, moved = pl.pallas_call(
        final_kernel,
        out_shape=(field, f32(3, 32, 16, 128)),
        in_specs=[ANY] * 5,
        out_specs=(ANY, ANY),
        scratch_shapes=[
            scratch(128, 16, 128),
            scratch(16, 128),
            scratch(96, 16, 128),
            scratch(192, 96),
            scratch(96, 128),
            scratch(192, 128),
            scratch(3, 32, 16, 128),
            pltpu.SemaphoreType.DMA((6,)),
            pltpu.SemaphoreType.DMA((3,)),
        ],
        compiler_params=pltpu.CompilerParams(vmem_limit_bytes=LIMIT),
        name="final",
    )(both, share, fresh, match, spread_z)
    return join(fresh), join(moved)


def solution(mesh):
    blocks = ("blk", "sub")
    placed = (
        P(blocks, None, None),
        P(blocks, None, None),
        P(blocks),
        P(blocks),
        P(blocks, None),
        P(blocks),
        P(blocks, None),
        P(blocks, None),
    )
    return jax.shard_map(
        body,
        mesh=mesh,
        in_specs=placed,
        out_specs=(P(blocks, None, None), P(blocks, None, None)),
        check_vma=False,
    )
```

```python
import math

import jax
import jax.numpy as jnp
import ml_dtypes
import numpy as np
from jax import lax
from jax.experimental import pallas as pl
from jax.experimental.pallas import tpu as pltpu
from jax.sharding import PartitionSpec as P

MESH = pl.DeviceIdType.MESH
RINGS = 32
MATES = (2, 3, 4, 5, 6, 7, 1)
STEPS_Z = (4, 3, 5, 2, 6, 1, 7)
STEPS_Y = (2, 1, 3)
GX = 32
GY = 128
GZ = 4


def fold_tables():
    row = np.arange(192)
    lane = np.arange(128)
    n = np.arange(256)
    row_c_ix, row_iy, row_b = row // 16, (row % 16) // 4, row % 2
    lane_iz = (lane % 32) // 8
    live = n < 192
    fold = ((lane_iz[:, None] == n[None, :] % 4) & live[None, :]) * 1.0
    pick = ((n[None, :] // 4 == (row_iy * 12 + row_c_ix)[:, None]) & live[None, :]) * 1.0
    mean = (np.arange(8)[:, None] == row_b[None, :]) / 512.0
    return fold.astype(np.float32), pick.astype(np.float32), mean.astype(np.float32)


def iota(shape, dim):
    return lax.broadcasted_iota(jnp.int32, shape, dim)


def place():
    blk, sub = lax.axis_index("blk"), lax.axis_index("sub")
    return blk // 2, lax.rem(blk, 2), sub


def row_pair(first, second):
    return jnp.where((iota((8, 128), 0) & 1) == 0, first, second)


class Chunk:
    def __init__(self, first, count, s1, r1, s2, r2, sem):
        self.first, self.count = first, count
        self.s1, self.r1, self.s2, self.r2, self.sem = s1, r1, s2, r2, sem
        self.rows = 12 * count

    def at(self, b, f, c):
        return (b * self.count + f - self.first) * 6 + c

    def put(self, b, f, c, plane):
        self.s1[pl.ds(self.at(b, f, c), 8, stride=self.rows), :] = plane

    def own(self, b, f, c):
        return self.s1[pl.ds(self.at(b, f, c), 8, stride=self.rows), :]

    def ghost(self, b, f, c):
        return self.r2[pl.ds(self.at(b, f, c), 8, stride=self.rows), :]

    def piece(self, which, count=1):
        return pl.ds(pl.multiple_of(which * self.rows, 8), count * self.rows)


def front_kernel(nb_ref, level_ref, owner_ref, speed_ref, slot_hbm, *refs):
    sources, (fresh_hbm, both_hbm, share_hbm), refs = refs[:11], refs[11:14], refs[14:]
    held, refs = refs[:11], refs[11:]
    wv, uv, solid, fold_ref, pick_ref, mean_ref, inv_xz, inv_y, fwd_y, fwd_xz, spectral = held
    (out_ref, both, s1a, r1a, s2a, r2a, s1b, r1b, s2b, r2b, tmp, nbs, nbr, acc, t1, g, chosen, near_y, mine_s, peer_s, share_s,
     slot_ref, in_sem, out_sem, ssem, rsem) = refs
    ring, half, sub = place()
    me = half * 4 + sub
    y, z = ring // 8, lax.rem(ring, 8)
    loads = [pltpu.make_async_copy(src, dst, in_sem.at[n]) for n, (src, dst) in enumerate(zip(sources, held))]
    loads.append(pltpu.make_async_copy(slot_hbm, slot_ref, in_sem.at[11]))
    for load in loads:
        load.start()

    def mate(k):
        other = lax.bitwise_xor(me, k)
        return (ring * 2 + other // 4, lax.rem(other, 4))

    def beside(step):
        return (lax.rem(ring + step + RINGS, RINGS) * 2 + half, sub)

    def along_z(k):
        return ((y * 8 + lax.rem(z + k, 8)) * 2 + half, sub)

    def along_y(k):
        return ((lax.rem(y + k, 4) * 8 + z) * 2 + half, sub)

    mates = [mate(k) for k in MATES]
    on_z = [along_z(k) for k in STEPS_Z]
    on_y = [along_y(k) for k in STEPS_Y]
    everyone = mates + [beside(1), beside(-1)] + on_z + on_y
    barrier = pltpu.get_barrier_semaphore()
    for device in everyone:
        pl.semaphore_signal(barrier, inc=1, device_id=device, device_id_type=MESH)

    lane = iota((8, 128), 1)
    row = iota((8, 128), 0)
    wants = jnp.zeros((8, 128), jnp.int32)
    for b in range(2):
        for f in range(6):
            wants = jnp.where(lane == b * 6 + f, nb_ref[b, f] + half * 8, wants)
        wants = jnp.where(lane == 12 + b, owner_ref[b], wants)
    nbs[...] = wants
    nbr[pl.ds(pl.multiple_of(me * 8, 8), 8), :] = wants
    for load in loads[:2]:
        load.wait()

    flat = (wv.reshape(1536, 128), uv.reshape(1536, 128))

    def source(c):
        return flat[c // 3], (c % 3) * 512

    def remote(src, dst, sem, device):
        return pltpu.make_async_remote_copy(
            src_ref=src, dst_ref=dst, send_sem=ssem.at[sem], recv_sem=rsem.at[sem],
            device_id=device, device_id_type=MESH)

    def start(copies):
        for copy in copies:
            copy.start()
        return copies

    def finish(copies):
        for copy in copies:
            copy.wait()

    xy = Chunk(0, 4, s1a, r1a, s2a, r2a, 8)
    zz = Chunk(4, 2, s1b, r1b, s2b, r2b, 24)

    def scatter_faces(part):
        copies = start([
            remote(part.s1.at[part.piece(lax.bitwise_xor(me, k))], part.r1.at[part.piece(4 + me)], part.sem + k - 1, mate(k))
            for k in MATES
        ])
        part.r1[part.piece(4 + me), :] = part.s1[part.piece(me), :]
        return copies

    def forward_faces(part):
        return start([
            remote(part.r1.at[part.piece(8, 4)], part.r1.at[part.piece(0, 4)], part.sem + 7, beside(1)),
            remote(part.r1.at[part.piece(4, 4)], part.r1.at[part.piece(12, 4)], part.sem + 8, beside(-1)),
        ])

    def return_faces(part):
        copies = start([
            remote(part.s2.at[part.piece(lax.bitwise_xor(me, k))], part.r2.at[part.piece(me)], part.sem + 8 + k, mate(k))
            for k in MATES
        ])
        part.r2[part.piece(me), :] = part.s2[part.piece(me), :]
        return copies

    for c in range(6):
        ref, base = source(c)
        for b in range(2):
            for f, x in ((0, 0), (1, 31)):
                xy.put(b, f, c, ref[pl.ds(base + x * 16 + b, 8, stride=2), :])
            low = high = jnp.zeros((8, 128), jnp.float32)
            for n in range(4):
                first = ref[pl.ds(base + n * 128 + b, 8, stride=16), :]
                last = ref[pl.ds(base + n * 128 + 14 + b, 8, stride=16), :]
                if n:
                    first = pltpu.roll(first, 32 * n, 1)
                if n != 3:
                    last = pltpu.roll(last, (32 * n + 32) % 128, 1)
                here = lane // 32 == n
                low = jnp.where(here, first, low)
                high = jnp.where(here, last, high)
            xy.put(b, 2, c, low)
            xy.put(b, 3, c, high)

    pl.semaphore_wait(barrier, len(everyone))
    mine = pl.ds(pl.multiple_of(me * 8, 8), 8)
    sent_wants = start([remote(nbs, nbr.at[mine], k - 1, mate(k)) for k in MATES])
    sent_xy = scatter_faces(xy)

    def gather_z(x, held):
        at_low = (lane & 31) == x
        at_high = (lane & 31) == ((x + 31) & 31)
        fresh = []
        for c in range(6):
            ref, base = source(c)
            for h in range(2):
                plane = ref[pl.ds(pl.multiple_of(base + x * 16 + h * 8, 8), 8), :]
                turned = pltpu.roll(plane, x, 1)
                low, high = held[(c * 2 + h) * 2], held[(c * 2 + h) * 2 + 1]
                fresh += [jnp.where(at_low, turned, low), jnp.where(at_high, turned, high)]
        return tuple(fresh)

    zero = jnp.zeros((8, 128), jnp.float32)
    packed = lax.fori_loop(0, 32, gather_z, (zero,) * 24)
    for c in range(6):
        for which in range(2):
            for h in range(2):
                at = (c * 2 + which) * 16 + h * 8
                plane = packed[(c * 2 + h) * 2 + which]
                tmp[at : at + 8, :] = pltpu.roll(plane, 97, 1) if which else plane
    for c in range(6):
        for which in range(2):
            for b in range(2):
                zz.put(b, 4 + which, c, tmp[pl.ds((c * 2 + which) * 16 + b, 8, stride=2), :])
    sent_zz = scatter_faces(zz)

    def scale(level):
        return lax.shift_left(1, level).astype(jnp.float32)

    sizes = [scale(level_ref[b]) for b in range(2)]
    slopes_of = [0.05 * 0.5 * size for size in sizes]
    spread_of = [0.05 * 0.1 * (size * size) for size in sizes]
    slope = row_pair(*slopes_of)
    spread = row_pair(*spread_of)

    def around(x, c, h):
        ref = (wv, uv)[c // 3]
        at = (c % 3) * 32 + x
        rows = slice(h * 8, h * 8 + 8)
        here = ref[at, rows, :]
        left = jnp.zeros_like(here) if isinstance(x, int) and x == 0 else ref[at - 1, rows, :]
        right = jnp.zeros_like(here) if isinstance(x, int) and x == 31 else ref[at + 1, rows, :]
        if h == 0:
            before = jnp.where(row < 2, 0.0, pltpu.roll(here, 2, 0))
            after = ref[at, 2:10, :]
        else:
            before = ref[at, 6:14, :]
            after = jnp.where(row >= 6, 0.0, pltpu.roll(here, 6, 0))
        before = pltpu.roll(jnp.where(lane >= 96, before, here), 32, 1)
        after = pltpu.roll(jnp.where(lane < 32, after, here), 96, 1)
        below = jnp.where((lane & 31) == 0, 0.0, pltpu.roll(here, 1, 1))
        above = jnp.where((lane & 31) == 31, 0.0, pltpu.roll(here, 127, 1))
        return here, (left, right), (before, after), (below, above)

    def plane(x):
        for h in range(2):
            parts = [around(x, c, h) for c in range(6)]
            heres = [part[0] for part in parts]
            slopes = [[part[1 + d][1] - part[1 + d][0] for d in range(3)] for part in parts]
            for i in range(3):
                turn = heres[0] * slopes[3 + i][0] + heres[1] * slopes[3 + i][1] + heres[2] * slopes[3 + i][2]
                turn -= heres[3] * slopes[i][0] + heres[4] * slopes[i][1] + heres[5] * slopes[i][2]
                ends = [part for d in range(3) for part in parts[i][1 + d]]
                total = (ends[0] + ends[1]) + (ends[2] + ends[3]) + (ends[4] + ends[5])
                out_ref[i * 32 + x, h * 8 : h * 8 + 8, :] = (
                    heres[i] + slope * turn + spread * (total - 6.0 * heres[i])
                )

    def planes(low, high):
        def step(x, carry):
            plane(x)
            return carry

        lax.fori_loop(low, high, step, 0)

    plane(0)
    planes(1, 15)
    finish(sent_wants)
    finish(sent_xy)
    sent_xy = forward_faces(xy)
    planes(15, 23)
    finish(sent_zz)
    sent_zz = forward_faces(zz)
    planes(23, 31)
    plane(31)

    slot = iota((8, 96), 1) & 31
    dead_low = (ring == 0).astype(jnp.int32)
    dead_high = (ring == RINGS - 1).astype(jnp.int32)
    alive = 1 - dead_low * (slot < 8).astype(jnp.int32) - dead_high * (slot >= 24).astype(jnp.int32)
    alive = alive.astype(jnp.float32)

    def select(part):
        wanted = nbr[pl.ds(0, 8, stride=8), :]
        for f in range(part.first, part.first + part.count):
            hot = jnp.concatenate(
                [jnp.where(wanted[:, b * 6 + f : b * 6 + f + 1] == slot, alive, 0.0) for b in range(2)], axis=0)
            data = jnp.concatenate(
                [part.r1[pl.ds(part.at(0, f ^ 1, c), 32, stride=6 * part.count), :] for c in range(6)], axis=1)
            hot = hot.astype(jnp.bfloat16)
            got = dot(hot, jnp.concatenate(thirds(data), axis=0))
            for b in range(2):
                for c in range(6):
                    part.s2[pl.ds(part.at(b, f, c), 8, stride=part.rows), :] = (
                        got[b * 8 : b * 8 + 8, c * 128 : c * 128 + 128]
                    )

    finish(sent_xy)
    select(xy)
    sent_xy = return_faces(xy)
    finish(sent_zz)
    select(zz)
    sent_zz = return_faces(zz)

    moved = out_ref.reshape(1536, 128)

    def added(part, b, f):
        ghosts = [part.ghost(b, f, c) for c in range(6)]
        vort, veloc = part.own(b, f, f // 2), part.own(b, f, 3 + f // 2)
        sign = slopes_of[b] * (1.0 if f % 2 else -1.0)
        vort, veloc = vort * sign, spread_of[b] - veloc * sign
        return [vort * ghosts[3 + i] + veloc * ghosts[i] for i in range(3)]

    finish(sent_xy)
    for b in range(2):
        for f, x in ((0, 0), (1, 31)):
            for i, extra in enumerate(added(xy, b, f)):
                moved[pl.ds(i * 512 + x * 16 + b, 8, stride=2), :] += extra
        for f, at, zone in ((2, 0, 0), (3, 14, 3)):
            for i, extra in enumerate(added(xy, b, f)):
                for n in range(4):
                    turn = (32 * (zone - n)) % 128
                    part = pltpu.roll(extra, turn, 1) if turn else extra
                    moved[pl.ds(i * 512 + n * 128 + at + b, 8, stride=16), :] += jnp.where(lane // 32 == zone, part, 0.0)
    finish(sent_zz)
    for b in range(2):
        for which in range(2):
            for i, extra in enumerate(added(zz, b, 4 + which)):
                tmp[pl.ds((i * 2 + which) * 16 + b, 8, stride=2), :] = extra
    ends = [[tmp[n * 16 + h * 8 : n * 16 + h * 8 + 8, :] for h in range(2)] for n in range(6)]

    def close(ix, carry):
        sums = [jnp.zeros((8, 128), jnp.float32)] * 6
        for step in range(8):
            x = ix * 8 + step
            for i in range(3):
                for h in range(2):
                    low = pltpu.roll(ends[i * 2][h], (128 - x) & 127, 1)
                    high = pltpu.roll(ends[i * 2 + 1][h], (159 - x) & 127, 1)
                    extra = jnp.where((lane & 31) == 0, low, jnp.where((lane & 31) == 31, high, 0.0))
                    fresh = out_ref[i * 32 + x, h * 8 : h * 8 + 8, :] + extra
                    out_ref[i * 32 + x, h * 8 : h * 8 + 8, :] = fresh
                    sums[i * 2 + h] = sums[i * 2 + h] + fresh
        for i in range(3):
            for h in range(2):
                acc[pl.ds(pl.multiple_of((i * 4 + ix) * 16 + h * 8, 8), 8), :] = sums[i * 2 + h]
        return carry

    lax.fori_loop(0, 4, close, 0)

    stores = [pltpu.make_async_copy(out_ref, fresh_hbm, out_sem.at[0])]
    stores[0].start()
    for load in loads[2:]:
        load.wait()
    fold, mean = fold_ref[...].astype(jnp.bfloat16), mean_ref[...].astype(jnp.bfloat16)
    folded = sum(dot(part, fold) for part in thirds(acc[...])) * pick_ref[...]
    rows = sum(dot(mean, part) for part in thirds(folded))
    wide_row, wide_lane = iota((8, 256), 0), iota((8, 256), 1)

    def shrink(level):
        return jnp.where(level == 0, 1.0, jnp.where(level == 1, 0.125, 0.015625))

    rows = rows * jnp.where(wide_row == 0, shrink(level_ref[0]), shrink(level_ref[1]))
    owners = jnp.where(wide_row == 0, owner_ref[0], owner_ref[1]).astype(jnp.float32)
    rows = jnp.where(wide_lane == 192, owners, rows)
    gap = jnp.zeros((2, 128), jnp.float32)
    spot = half * 2 + sub // 2
    mine = pl.ds(pl.multiple_of(spot * 8, 8), 8)
    t1[mine, :] = jnp.concatenate(
        [rows[0:1, 0:128], rows[0:1, 128:256], gap, rows[1:2, 0:128], rows[1:2, 128:256], gap], axis=0)

    def share(ref, targets, first):
        return start([remote(ref, ref, first + n, device) for n, device in enumerate(targets)])

    sent = share(t1.at[mine], [mate(k) for k in (2, 4, 6)], 40)

    on = [jnp.where(slot_ref[0] == b, 10.0, 0.0) for b in range(2)]
    flat_both = both.reshape(2048, 128)

    def penalise(x, carry):
        part = solid[pl.ds(pl.multiple_of(x * 8, 8), 8), :]
        at = (x // 16) * 64 + lax.rem(x, 16)
        for b in range(2):
            flat_both[pl.ds((at + 48) * 16 + b, 8, stride=2), :] = part * on[b]
        for h in range(2):
            rows = slice(h * 8, h * 8 + 8)
            chi = both[at + 48, rows, :]
            scale = 1.0 / (1.0 + chi)
            both[at + 48, rows, :] = scale
            for c in range(3):
                both[at + c * 16, rows, :] = (uv[c * 32 + x, rows, :] + chi * speed_ref[0, c]) * scale
        return carry

    lax.fori_loop(0, 32, penalise, 0)
    stores += start([pltpu.make_async_copy(both, both_hbm, out_sem.at[1])])
    finish(sent)
    first = ring * 8
    at = pl.ds(pl.multiple_of(first, 8), 8)
    for t in range(2):
        g[at, t * 128 : t * 128 + 128] = t1[pl.ds(t, 8, stride=4), :]
    sent = share(g.at[at], on_z, 43)

    theirs = nbr[pl.ds(pl.multiple_of(lax.bitwise_xor(me, 1) * 8, 8), 8), :]
    owners = [jnp.full((8, 128), owner_ref[b], jnp.int32) for b in range(2)]
    owners += [jnp.broadcast_to(theirs[:, 12 + b : 13 + b], (8, 128)) for b in range(2)]
    columns = [owner & 31 for owner in owners]
    bands = [owner // 32 for owner in owners]

    def pick_y(py, carry):
        found = []
        for n in range(2):
            row_of = inv_y[pl.ds(pl.multiple_of(py * 8, 8), 8), n * 128 : n * 128 + 128]
            found += [jnp.where(columns[k] == py, row_of, carry[n * 4 + k]) for k in range(4)]
        return tuple(found)

    for n, part in enumerate(lax.fori_loop(0, 32, pick_y, (zero,) * 8)):
        near_y[pl.ds((n % 4 // 2) * 32 + (n // 4) * 16 + n % 2, 8, stride=2), :] = part

    def pick_xz(px, carry):
        found = []
        for n in range(4):
            row_of = inv_xz[pl.ds(pl.multiple_of((n // 2) * 128 + px * 16 + (n % 2) * 8, 8), 8), :]
            found += [jnp.where(bands[k] == px, row_of, carry[n * 4 + k]) for k in range(4)]
        return tuple(found)

    for n, part in enumerate(lax.fori_loop(0, 8, pick_xz, (zero,) * 16)):
        k, n = n % 4, n // 4
        to = (k // 2) * 64 + (n // 2) * 32 + (k % 2) * 16 + (n % 2) * 8
        chosen[to : to + 8, :] = part
    finish(sent)
    finish(share(g.at[pl.ds(pl.multiple_of(y * 64, 64), 64)], on_y, 50))

    own, other = solve(g[...], fwd_y, fwd_xz, spectral, chosen, near_y)
    mine_s[:, 0:96] = other
    sent = start([remote(mine_s, peer_s, 53, mate(1))])
    finish(sent)
    share_s[:, 0:96] = own + peer_s[:, 0:96]
    stores += start([pltpu.make_async_copy(share_s, share_hbm, out_sem.at[2])])
    finish(stores)


def halves(table):
    high = table.astype(ml_dtypes.bfloat16).astype(np.float64)
    low = (table - high).astype(ml_dtypes.bfloat16).astype(np.float64)
    return high, low


def solve_tables():
    space = np.arange(128)
    px, ix, iz = space // 16, (space // 4) % 4, space % 4
    x, z = 4 * px + ix, iz
    kx, kz = space // 4, space % 4
    iy, py = space // 32, space % 32
    y = 4 * py + iy
    ky = space
    theta = 2.0 * np.pi * ((kx[:, None] * x[None, :] % 32) / 32.0 + (kz[:, None] * z[None, :] % 4) / 4.0)
    phi = 2.0 * np.pi * ((y[:, None] * ky[None, :]) % 128) / 128.0
    high, low = halves(np.concatenate([np.cos(phi), -np.sin(phi)], axis=1))
    fwd_y = np.concatenate([high, high, low], axis=0)
    high, low = halves(np.concatenate([np.cos(theta), np.sin(theta)], axis=0))
    fwd_xz = np.concatenate([high, low], axis=1)
    inv_xz = np.concatenate([np.cos(theta.T), np.sin(theta.T)], axis=0).astype(np.float32)
    line = np.arange(256)
    turn = 2.0 * np.pi * (((4 * (line // 8) + (line % 8) // 2)[:, None] * ky[None, :]) % 128) / 128.0
    inv_y = (np.concatenate([np.cos(turn), -np.sin(turn)], axis=1) / 16384.0).astype(np.float32)

    def waves(index, length):
        signed = np.where(index < (length + 1) // 2, index, index - length)
        full = signed * (2.0 * math.pi / length)
        return full, np.where(index == length // 2, 0.0, full)

    full_x, slope_x = waves(kx, GX)
    full_y, slope_y = waves(ky, GY)
    full_z, slope_z = waves(kz, GZ)
    square = (full_x**2 + full_z**2)[:, None] + (full_y**2)[None, :]
    inverse = np.where(square > 0, 1.0 / np.where(square > 0, square, 1.0), 0.0)
    spectral = np.concatenate([inverse * slope_x[:, None], inverse * slope_y[None, :], inverse * slope_z[:, None]])
    src = np.arange(96)
    row = np.arange(192)
    src_c, src_b, src_ix, src_iz = src // 32, (src // 16) % 2, (src // 4) % 4, src % 4
    match = ((src_c * 4 + src_ix)[None, :] == (row // 16)[:, None]) & (src_b[None, :] == (row % 2)[:, None])
    spread_z = src_iz[:, None] == ((np.arange(128) % 32) // 8)[None, :]
    return tuple(a.astype(np.float32) for a in (inv_xz, inv_y, fwd_y, fwd_xz, spectral, match * 1.0, spread_z * 1.0))


def cut(array):
    high = array.astype(jnp.bfloat16)
    return high, (array - high.astype(jnp.float32)).astype(jnp.bfloat16)


def thirds(array):
    high = array.astype(jnp.bfloat16)
    rest = array - high.astype(jnp.float32)
    middle = rest.astype(jnp.bfloat16)
    return high, middle, (rest - middle.astype(jnp.float32)).astype(jnp.bfloat16)


def dot(left, right):
    return jnp.dot(left, right, preferred_element_type=jnp.float32)


def dot_nt(left, right):
    return lax.dot_general(left, right, (((1,), (1,)), ((), ())), preferred_element_type=jnp.float32)


def solve(sent, fwd_y, fwd_xz, spectral, chosen, near_y):
    hot = (sent[:, 192:193] == iota((256, 256), 1).astype(jnp.float32)).astype(jnp.bfloat16)
    high, low = cut(sent.T)
    columns = dot(high, hot) + dot(low, hot)
    lane = iota((48, 128), 1)
    rows = []
    for px in range(8):
        held = None
        for iy in range(4):
            part = columns[iy * 48 : iy * 48 + 48, (px // 4) * 128 : (px // 4) * 128 + 128]
            turn = ((iy - px % 4) * 32) % 128
            if turn:
                part = pltpu.roll(part, turn, 1)
            held = part if held is None else jnp.where(lane >= iy * 32, part, held)
        rows.append(held)
    high, low = cut(jnp.concatenate(rows, axis=0))
    table = fwd_y[...].astype(jnp.bfloat16)
    waves_y = dot(jnp.concatenate([high, low], axis=1), table[0:256]) + dot(high, table[256:384])
    stacked = jnp.concatenate(
        [
            jnp.concatenate([waves_y[px * 48 + c * 16 : px * 48 + c * 16 + 16, :] for px in range(8)], axis=0)
            for c in range(3)
        ],
        axis=1,
    )
    high, low = cut(stacked)
    table = fwd_xz[...].astype(jnp.bfloat16)
    full = dot(table, jnp.concatenate([high, high], axis=0)) + dot(table[:, 0:128], low)
    slope_x, slope_y, slope_z = spectral[0:128, :], spectral[128:256, :], spectral[256:384, :]
    real, imag = [], []
    for c in range(3):
        low = full[:, c * 256 : c * 256 + 128]
        high = full[:, c * 256 + 128 : c * 256 + 256]
        real.append(low[0:128] + high[128:256])
        imag.append(high[0:128] - low[128:256])

    def cross(hat):
        return [
            slope_y * hat[2] - slope_z * hat[1],
            slope_z * hat[0] - slope_x * hat[2],
            slope_x * hat[1] - slope_y * hat[0],
        ]

    cross_real, cross_imag = cross(real), cross(imag)
    high, low = cut(jnp.concatenate([part for c in range(3) for part in (-cross_imag[c], cross_real[c])], axis=1))
    chosen_high, chosen_low = cut(chosen[...])
    near = dot(jnp.concatenate([chosen_high, chosen_low], axis=1), jnp.concatenate([high, high], axis=0))
    near = near + dot(chosen_high, low)
    shares = []
    for side in range(2):
        lines = []
        for c in range(3):
            low = near[side * 64 : side * 64 + 64, c * 256 : c * 256 + 128]
            high = near[side * 64 : side * 64 + 64, c * 256 + 128 : c * 256 + 256]
            lines.append(jnp.concatenate([low[0:32] - high[32:64], high[0:32] + low[32:64]], axis=1))
        high, low = cut(jnp.concatenate(lines, axis=0))
        near_high, near_low = cut(jnp.concatenate([near_y[side * 32 + n * 16 : side * 32 + n * 16 + 16, :] for n in range(2)], axis=1))
        shares.append(dot_nt(near_high, high) + (dot_nt(near_high, low) + dot_nt(near_low, high)))
    return shares


def lift(share, match, spread_z):
    high, low = cut(jnp.concatenate([share] * 12, axis=0) * match[...])
    table = spread_z[...].astype(jnp.bfloat16)
    return dot(high, table) + dot(low, table)


def final_kernel(both_hbm, share_hbm, fresh_hbm, match_hbm, spread_hbm, fresh_out, out_hbm,
                 both, share, fresh, match, spread_z, field, moved, sem, out_sem):
    halves_of = [pl.ds(n * 64, 64) for n in range(2)]
    loads = [pltpu.make_async_copy(share_hbm, share, sem.at[0])]
    loads += [pltpu.make_async_copy(both_hbm.at[part], both.at[part], sem.at[1 + n]) for n, part in enumerate(halves_of)]
    loads += [pltpu.make_async_copy(fresh_hbm, fresh, sem.at[3])]
    tables = [pltpu.make_async_copy(match_hbm, match, sem.at[4]), pltpu.make_async_copy(spread_hbm, spread_z, sem.at[5])]
    for load in loads[:1] + tables + loads[1:]:
        load.start()
    for load in loads[:1] + tables:
        load.wait()
    field[...] = lift(share[:, 0:96], match, spread_z)
    stores = []
    for n in range(2):
        loads[1 + n].wait()
        for ix in (n * 2, n * 2 + 1):
            lifted = [[field[(c * 4 + ix) * 16 + h * 8 : (c * 4 + ix) * 16 + h * 8 + 8, :] for h in range(2)] for c in range(3)]
            for x in range(ix * 8, ix * 8 + 8):
                at = n * 64 + x % 16
                for h in range(2):
                    rows = slice(h * 8, h * 8 + 8)
                    scale = both[at + 48, rows, :]
                    for c in range(3):
                        moved[c, x, rows, :] = both[at + c * 16, rows, :] + lifted[c][h] * scale
        planes = pl.ds(n * 16, 16)
        stores.append(pltpu.make_async_copy(moved.at[:, planes], out_hbm.at[:, planes], out_sem.at[n]))
        stores[-1].start()
    loads[3].wait()
    stores.append(pltpu.make_async_copy(fresh, fresh_out, out_sem.at[2]))
    stores[-1].start()
    for copy in stores:
        copy.wait()


SMEM = pl.BlockSpec(memory_space=pltpu.SMEM)
ANY = pl.BlockSpec(memory_space=pl.ANY)
LIMIT = 62 * 2**20


def f32(*shape):
    return jax.ShapeDtypeStruct(shape, jnp.float32)


def scratch(*shape):
    return pltpu.VMEM(shape, jnp.float32)


def split(array):
    return array.reshape(2, 3, 256, 128).transpose(1, 2, 0, 3)


def join(array):
    return array.reshape(3, 256, 2, 128).transpose(2, 0, 1, 3).reshape(2, 3, 32768)


def body(vorticity, velocity, level_map, patch_owner, neighbours, fish_slot, fish_mask, fish_speed):
    w, u = split(vorticity), split(velocity)
    w, u = w.reshape(96, 16, 128), u.reshape(96, 16, 128)
    field = f32(96, 16, 128)

    def faces(count):
        return [scratch(rows * count, 128) for rows in (96, 192, 96, 96)]

    *tables, match, spread_z = (jnp.asarray(a) for a in fold_tables() + solve_tables())
    sources = (w, u, fish_mask.reshape(256, 128), *tables)
    fresh, both, share = pl.pallas_call(
        front_kernel,
        out_shape=(field, f32(128, 16, 128), f32(16, 128)),
        in_specs=[SMEM] * 4 + [ANY] * 12,
        out_specs=(ANY,) * 3,
        scratch_shapes=[
            *(scratch(*array.shape) for array in sources),
            scratch(96, 16, 128),
            scratch(128, 16, 128),
            *faces(4),
            *faces(2),
            scratch(192, 128),
            pltpu.VMEM((8, 128), jnp.int32),
            pltpu.VMEM((64, 128), jnp.int32),
            scratch(192, 128),
            scratch(32, 128),
            scratch(256, 256),
            scratch(128, 128),
            scratch(64, 128),
            scratch(16, 128),
            scratch(16, 128),
            scratch(16, 128),
            pltpu.SMEM((1,), jnp.int32),
            pltpu.SemaphoreType.DMA((12,)),
            pltpu.SemaphoreType.DMA((3,)),
            pltpu.SemaphoreType.DMA((56,)),
            pltpu.SemaphoreType.DMA((56,)),
        ],
        compiler_params=pltpu.CompilerParams(collective_id=0, has_side_effects=True, vmem_limit_bytes=LIMIT),
        name="front",
    )(neighbours, level_map, patch_owner, fish_speed, fish_slot, *sources)
    fresh, moved = pl.pallas_call(
        final_kernel,
        out_shape=(field, f32(3, 32, 16, 128)),
        in_specs=[ANY] * 5,
        out_specs=(ANY, ANY),
        scratch_shapes=[
            scratch(128, 16, 128),
            scratch(16, 128),
            scratch(96, 16, 128),
            scratch(192, 96),
            scratch(96, 128),
            scratch(192, 128),
            scratch(3, 32, 16, 128),
            pltpu.SemaphoreType.DMA((6,)),
            pltpu.SemaphoreType.DMA((3,)),
        ],
        compiler_params=pltpu.CompilerParams(vmem_limit_bytes=LIMIT),
        name="final",
    )(both, share, fresh, match, spread_z)
    return join(fresh), join(moved)


def solution(mesh):
    blocks = ("blk", "sub")
    placed = (
        P(blocks, None, None),
        P(blocks, None, None),
        P(blocks),
        P(blocks),
        P(blocks, None),
        P(blocks),
        P(blocks, None),
        P(blocks, None),
    )
    return jax.shard_map(
        body,
        mesh=mesh,
        in_specs=placed,
        out_specs=(P(blocks, None, None), P(blocks, None, None)),
        check_vma=False,
    )
```

```python
import math

import jax
import jax.numpy as jnp
import ml_dtypes
import numpy as np
from jax import lax
from jax.experimental import pallas as pl
from jax.experimental.pallas import tpu as pltpu
from jax.sharding import PartitionSpec as P

MESH = pl.DeviceIdType.MESH
RINGS = 32
MATES = (2, 3, 4, 5, 6, 7, 1)
STEPS_Z = (4, 3, 5, 2, 6, 1, 7)
STEPS_Y = (2, 1, 3)
GX = 32
GY = 128
GZ = 4


def fold_tables():
    row = np.arange(192)
    lane = np.arange(128)
    n = np.arange(256)
    row_c_ix, row_iy, row_b = row // 16, (row % 16) // 4, row % 2
    lane_iz = (lane % 32) // 8
    live = n < 192
    fold = ((lane_iz[:, None] == n[None, :] % 4) & live[None, :]) * 1.0
    pick = ((n[None, :] // 4 == (row_iy * 12 + row_c_ix)[:, None]) & live[None, :]) * 1.0
    mean = (np.arange(8)[:, None] == row_b[None, :]) / 512.0
    return fold.astype(np.float32), pick.astype(np.float32), mean.astype(np.float32)


def iota(shape, dim):
    return lax.broadcasted_iota(jnp.int32, shape, dim)


def place():
    blk, sub = lax.axis_index("blk"), lax.axis_index("sub")
    return blk // 2, lax.rem(blk, 2), sub


def row_pair(first, second):
    return jnp.where((iota((8, 128), 0) & 1) == 0, first, second)


class Chunk:
    def __init__(self, first, count, s1, r1, s2, r2, sem):
        self.first, self.count = first, count
        self.s1, self.r1, self.s2, self.r2, self.sem = s1, r1, s2, r2, sem
        self.rows = 12 * count

    def at(self, b, f, c):
        return (b * self.count + f - self.first) * 6 + c

    def put(self, b, f, c, plane):
        self.s1[pl.ds(self.at(b, f, c), 8, stride=self.rows), :] = plane

    def own(self, b, f, c):
        return self.s1[pl.ds(self.at(b, f, c), 8, stride=self.rows), :]

    def ghost(self, b, f, c):
        return self.r2[pl.ds(self.at(b, f, c), 8, stride=self.rows), :]

    def piece(self, which, count=1):
        return pl.ds(pl.multiple_of(which * self.rows, 8), count * self.rows)


def front_kernel(nb_ref, level_ref, owner_ref, speed_ref, slot_hbm, *refs):
    sources, (fresh_hbm, both_hbm, share_hbm), refs = refs[:11], refs[11:14], refs[14:]
    held, refs = refs[:11], refs[11:]
    wv, uv, solid, fold_ref, pick_ref, mean_ref, inv_xz, inv_y, fwd_y, fwd_xz, spectral = held
    (out_ref, both, s1a, r1a, s2a, r2a, s1b, r1b, s2b, r2b, tmp, nbs, nbr, acc, t1, g, chosen, near_y, mine_s, peer_s, share_s,
     slot_ref, in_sem, out_sem, ssem, rsem) = refs
    ring, half, sub = place()
    me = half * 4 + sub
    y, z = ring // 8, lax.rem(ring, 8)
    loads = [pltpu.make_async_copy(src, dst, in_sem.at[n]) for n, (src, dst) in enumerate(zip(sources, held))]
    loads.append(pltpu.make_async_copy(slot_hbm, slot_ref, in_sem.at[11]))
    for load in loads:
        load.start()

    def mate(k):
        other = lax.bitwise_xor(me, k)
        return (ring * 2 + other // 4, lax.rem(other, 4))

    def beside(step):
        return (lax.rem(ring + step + RINGS, RINGS) * 2 + half, sub)

    def along_z(k):
        return ((y * 8 + lax.rem(z + k, 8)) * 2 + half, sub)

    def along_y(k):
        return ((lax.rem(y + k, 4) * 8 + z) * 2 + half, sub)

    mates = [mate(k) for k in MATES]
    on_z = [along_z(k) for k in STEPS_Z]
    on_y = [along_y(k) for k in STEPS_Y]
    everyone = mates + [beside(1), beside(-1)] + on_z + on_y
    barrier = pltpu.get_barrier_semaphore()
    for device in everyone:
        pl.semaphore_signal(barrier, inc=1, device_id=device, device_id_type=MESH)

    lane = iota((8, 128), 1)
    row = iota((8, 128), 0)
    wants = jnp.zeros((8, 128), jnp.int32)
    for b in range(2):
        for f in range(6):
            wants = jnp.where(lane == b * 6 + f, nb_ref[b, f] + half * 8, wants)
        wants = jnp.where(lane == 12 + b, owner_ref[b], wants)
    nbs[...] = wants
    nbr[pl.ds(pl.multiple_of(me * 8, 8), 8), :] = wants
    for load in loads[:2]:
        load.wait()

    flat = (wv.reshape(1536, 128), uv.reshape(1536, 128))

    def source(c):
        return flat[c // 3], (c % 3) * 512

    def remote(src, dst, sem, device):
        return pltpu.make_async_remote_copy(
            src_ref=src, dst_ref=dst, send_sem=ssem.at[sem], recv_sem=rsem.at[sem],
            device_id=device, device_id_type=MESH)

    def start(copies):
        for copy in copies:
            copy.start()
        return copies

    leaving = []

    def finish(copies):
        for copy in copies:
            copy.wait_recv()
        leaving.extend(copies)

    def drain():
        for copy in leaving:
            copy.wait_send()
        leaving.clear()

    xy = Chunk(0, 4, s1a, r1a, s2a, r2a, 8)
    zz = Chunk(4, 2, s1b, r1b, s2b, r2b, 24)

    def scatter_faces(part):
        copies = start([
            remote(part.s1.at[part.piece(lax.bitwise_xor(me, k))], part.r1.at[part.piece(4 + me)], part.sem + k - 1, mate(k))
            for k in MATES
        ])
        part.r1[part.piece(4 + me), :] = part.s1[part.piece(me), :]
        return copies

    def forward_faces(part):
        return start([
            remote(part.r1.at[part.piece(8, 4)], part.r1.at[part.piece(0, 4)], part.sem + 7, beside(1)),
            remote(part.r1.at[part.piece(4, 4)], part.r1.at[part.piece(12, 4)], part.sem + 8, beside(-1)),
        ])

    def return_faces(part):
        copies = start([
            remote(part.s2.at[part.piece(lax.bitwise_xor(me, k))], part.r2.at[part.piece(me)], part.sem + 8 + k, mate(k))
            for k in MATES
        ])
        part.r2[part.piece(me), :] = part.s2[part.piece(me), :]
        return copies

    for c in range(6):
        ref, base = source(c)
        for b in range(2):
            for f, x in ((0, 0), (1, 31)):
                xy.put(b, f, c, ref[pl.ds(base + x * 16 + b, 8, stride=2), :])
            low = high = jnp.zeros((8, 128), jnp.float32)
            for n in range(4):
                first = ref[pl.ds(base + n * 128 + b, 8, stride=16), :]
                last = ref[pl.ds(base + n * 128 + 14 + b, 8, stride=16), :]
                if n:
                    first = pltpu.roll(first, 32 * n, 1)
                if n != 3:
                    last = pltpu.roll(last, (32 * n + 32) % 128, 1)
                here = lane // 32 == n
                low = jnp.where(here, first, low)
                high = jnp.where(here, last, high)
            xy.put(b, 2, c, low)
            xy.put(b, 3, c, high)

    pl.semaphore_wait(barrier, len(everyone))
    mine = pl.ds(pl.multiple_of(me * 8, 8), 8)
    sent_wants = start([remote(nbs, nbr.at[mine], k - 1, mate(k)) for k in MATES])
    sent_xy = scatter_faces(xy)

    def gather_z(x, held):
        at_low = (lane & 31) == x
        at_high = (lane & 31) == ((x + 31) & 31)
        fresh = []
        for c in range(6):
            ref, base = source(c)
            for h in range(2):
                plane = ref[pl.ds(pl.multiple_of(base + x * 16 + h * 8, 8), 8), :]
                turned = pltpu.roll(plane, x, 1)
                low, high = held[(c * 2 + h) * 2], held[(c * 2 + h) * 2 + 1]
                fresh += [jnp.where(at_low, turned, low), jnp.where(at_high, turned, high)]
        return tuple(fresh)

    zero = jnp.zeros((8, 128), jnp.float32)
    packed = lax.fori_loop(0, 32, gather_z, (zero,) * 24)
    for c in range(6):
        for which in range(2):
            for h in range(2):
                at = (c * 2 + which) * 16 + h * 8
                plane = packed[(c * 2 + h) * 2 + which]
                tmp[at : at + 8, :] = pltpu.roll(plane, 97, 1) if which else plane
    for c in range(6):
        for which in range(2):
            for b in range(2):
                zz.put(b, 4 + which, c, tmp[pl.ds((c * 2 + which) * 16 + b, 8, stride=2), :])
    sent_zz = scatter_faces(zz)

    def scale(level):
        return lax.shift_left(1, level).astype(jnp.float32)

    sizes = [scale(level_ref[b]) for b in range(2)]
    slopes_of = [0.05 * 0.5 * size for size in sizes]
    spread_of = [0.05 * 0.1 * (size * size) for size in sizes]
    slope = row_pair(*slopes_of)
    spread = row_pair(*spread_of)

    def around(x, c, h):
        ref = (wv, uv)[c // 3]
        at = (c % 3) * 32 + x
        rows = slice(h * 8, h * 8 + 8)
        here = ref[at, rows, :]
        left = jnp.zeros_like(here) if isinstance(x, int) and x == 0 else ref[at - 1, rows, :]
        right = jnp.zeros_like(here) if isinstance(x, int) and x == 31 else ref[at + 1, rows, :]
        if h == 0:
            before = jnp.where(row < 2, 0.0, pltpu.roll(here, 2, 0))
            after = ref[at, 2:10, :]
        else:
            before = ref[at, 6:14, :]
            after = jnp.where(row >= 6, 0.0, pltpu.roll(here, 6, 0))
        before = pltpu.roll(jnp.where(lane >= 96, before, here), 32, 1)
        after = pltpu.roll(jnp.where(lane < 32, after, here), 96, 1)
        below = jnp.where((lane & 31) == 0, 0.0, pltpu.roll(here, 1, 1))
        above = jnp.where((lane & 31) == 31, 0.0, pltpu.roll(here, 127, 1))
        return here, (left, right), (before, after), (below, above)

    def plane(x):
        for h in range(2):
            parts = [around(x, c, h) for c in range(6)]
            heres = [part[0] for part in parts]
            slopes = [[part[1 + d][1] - part[1 + d][0] for d in range(3)] for part in parts]
            for i in range(3):
                turn = heres[0] * slopes[3 + i][0] + heres[1] * slopes[3 + i][1] + heres[2] * slopes[3 + i][2]
                turn -= heres[3] * slopes[i][0] + heres[4] * slopes[i][1] + heres[5] * slopes[i][2]
                ends = [part for d in range(3) for part in parts[i][1 + d]]
                total = (ends[0] + ends[1]) + (ends[2] + ends[3]) + (ends[4] + ends[5])
                out_ref[i * 32 + x, h * 8 : h * 8 + 8, :] = (
                    heres[i] + slope * turn + spread * (total - 6.0 * heres[i])
                )

    def planes(low, high):
        def step(x, carry):
            plane(x)
            return carry

        lax.fori_loop(low, high, step, 0)

    plane(0)
    planes(1, 15)
    finish(sent_wants)
    finish(sent_xy)
    sent_xy = forward_faces(xy)
    planes(15, 23)
    finish(sent_zz)
    sent_zz = forward_faces(zz)
    planes(23, 31)
    plane(31)

    slot = iota((8, 96), 1) & 31
    dead_low = (ring == 0).astype(jnp.int32)
    dead_high = (ring == RINGS - 1).astype(jnp.int32)
    alive = 1 - dead_low * (slot < 8).astype(jnp.int32) - dead_high * (slot >= 24).astype(jnp.int32)
    alive = alive.astype(jnp.float32)

    def select(part):
        wanted = nbr[pl.ds(0, 8, stride=8), :]
        for f in range(part.first, part.first + part.count):
            hot = jnp.concatenate(
                [jnp.where(wanted[:, b * 6 + f : b * 6 + f + 1] == slot, alive, 0.0) for b in range(2)], axis=0)
            data = jnp.concatenate(
                [part.r1[pl.ds(part.at(0, f ^ 1, c), 32, stride=6 * part.count), :] for c in range(6)], axis=1)
            hot = hot.astype(jnp.bfloat16)
            got = dot(hot, jnp.concatenate(thirds(data), axis=0))
            for b in range(2):
                for c in range(6):
                    part.s2[pl.ds(part.at(b, f, c), 8, stride=part.rows), :] = (
                        got[b * 8 : b * 8 + 8, c * 128 : c * 128 + 128]
                    )

    finish(sent_xy)
    select(xy)
    sent_xy = return_faces(xy)
    finish(sent_zz)
    select(zz)
    sent_zz = return_faces(zz)

    moved = out_ref.reshape(1536, 128)

    def added(part, b, f):
        ghosts = [part.ghost(b, f, c) for c in range(6)]
        vort, veloc = part.own(b, f, f // 2), part.own(b, f, 3 + f // 2)
        sign = slopes_of[b] * (1.0 if f % 2 else -1.0)
        vort, veloc = vort * sign, spread_of[b] - veloc * sign
        return [vort * ghosts[3 + i] + veloc * ghosts[i] for i in range(3)]

    finish(sent_xy)
    for b in range(2):
        for f, x in ((0, 0), (1, 31)):
            for i, extra in enumerate(added(xy, b, f)):
                moved[pl.ds(i * 512 + x * 16 + b, 8, stride=2), :] += extra
        for f, at, zone in ((2, 0, 0), (3, 14, 3)):
            for i, extra in enumerate(added(xy, b, f)):
                for n in range(4):
                    turn = (32 * (zone - n)) % 128
                    part = pltpu.roll(extra, turn, 1) if turn else extra
                    moved[pl.ds(i * 512 + n * 128 + at + b, 8, stride=16), :] += jnp.where(lane // 32 == zone, part, 0.0)
    finish(sent_zz)
    for b in range(2):
        for which in range(2):
            for i, extra in enumerate(added(zz, b, 4 + which)):
                tmp[pl.ds((i * 2 + which) * 16 + b, 8, stride=2), :] = extra
    ends = [[tmp[n * 16 + h * 8 : n * 16 + h * 8 + 8, :] for h in range(2)] for n in range(6)]

    def close(ix, carry):
        sums = [jnp.zeros((8, 128), jnp.float32)] * 6
        for step in range(8):
            x = ix * 8 + step
            for i in range(3):
                for h in range(2):
                    low = pltpu.roll(ends[i * 2][h], (128 - x) & 127, 1)
                    high = pltpu.roll(ends[i * 2 + 1][h], (159 - x) & 127, 1)
                    extra = jnp.where((lane & 31) == 0, low, jnp.where((lane & 31) == 31, high, 0.0))
                    fresh = out_ref[i * 32 + x, h * 8 : h * 8 + 8, :] + extra
                    out_ref[i * 32 + x, h * 8 : h * 8 + 8, :] = fresh
                    sums[i * 2 + h] = sums[i * 2 + h] + fresh
        for i in range(3):
            for h in range(2):
                acc[pl.ds(pl.multiple_of((i * 4 + ix) * 16 + h * 8, 8), 8), :] = sums[i * 2 + h]
        return carry

    lax.fori_loop(0, 4, close, 0)

    stores = [pltpu.make_async_copy(out_ref, fresh_hbm, out_sem.at[0])]
    stores[0].start()
    for load in loads[2:]:
        load.wait()
    fold, mean = fold_ref[...].astype(jnp.bfloat16), mean_ref[...].astype(jnp.bfloat16)
    folded = sum(dot(part, fold) for part in thirds(acc[...])) * pick_ref[...]
    rows = sum(dot(mean, part) for part in thirds(folded))
    wide_row, wide_lane = iota((8, 256), 0), iota((8, 256), 1)

    def shrink(level):
        return jnp.where(level == 0, 1.0, jnp.where(level == 1, 0.125, 0.015625))

    rows = rows * jnp.where(wide_row == 0, shrink(level_ref[0]), shrink(level_ref[1]))
    owners = jnp.where(wide_row == 0, owner_ref[0], owner_ref[1]).astype(jnp.float32)
    rows = jnp.where(wide_lane == 192, owners, rows)
    gap = jnp.zeros((2, 128), jnp.float32)
    spot = half * 2 + sub // 2
    mine = pl.ds(pl.multiple_of(spot * 8, 8), 8)
    t1[mine, :] = jnp.concatenate(
        [rows[0:1, 0:128], rows[0:1, 128:256], gap, rows[1:2, 0:128], rows[1:2, 128:256], gap], axis=0)

    def share(ref, targets, first):
        return start([remote(ref, ref, first + n, device) for n, device in enumerate(targets)])

    sent = share(t1.at[mine], [mate(k) for k in (2, 4, 6)], 40)

    drain()

    on = [jnp.where(slot_ref[0] == b, 10.0, 0.0) for b in range(2)]
    flat_both = both.reshape(2048, 128)

    def penalise(x, carry):
        part = solid[pl.ds(pl.multiple_of(x * 8, 8), 8), :]
        at = (x // 16) * 64 + lax.rem(x, 16)
        for b in range(2):
            flat_both[pl.ds((at + 48) * 16 + b, 8, stride=2), :] = part * on[b]
        for h in range(2):
            rows = slice(h * 8, h * 8 + 8)
            chi = both[at + 48, rows, :]
            scale = 1.0 / (1.0 + chi)
            both[at + 48, rows, :] = scale
            for c in range(3):
                both[at + c * 16, rows, :] = (uv[c * 32 + x, rows, :] + chi * speed_ref[0, c]) * scale
        return carry

    lax.fori_loop(0, 32, penalise, 0)
    stores += start([pltpu.make_async_copy(both, both_hbm, out_sem.at[1])])
    finish(sent)
    first = ring * 8
    at = pl.ds(pl.multiple_of(first, 8), 8)
    for t in range(2):
        g[at, t * 128 : t * 128 + 128] = t1[pl.ds(t, 8, stride=4), :]
    sent = share(g.at[at], on_z, 43)

    drain()

    theirs = nbr[pl.ds(pl.multiple_of(lax.bitwise_xor(me, 1) * 8, 8), 8), :]
    owners = [jnp.full((8, 128), owner_ref[b], jnp.int32) for b in range(2)]
    owners += [jnp.broadcast_to(theirs[:, 12 + b : 13 + b], (8, 128)) for b in range(2)]
    columns = [owner & 31 for owner in owners]
    bands = [owner // 32 for owner in owners]

    def pick_y(py, carry):
        found = []
        for n in range(2):
            row_of = inv_y[pl.ds(pl.multiple_of(py * 8, 8), 8), n * 128 : n * 128 + 128]
            found += [jnp.where(columns[k] == py, row_of, carry[n * 4 + k]) for k in range(4)]
        return tuple(found)

    for n, part in enumerate(lax.fori_loop(0, 32, pick_y, (zero,) * 8)):
        near_y[pl.ds((n % 4 // 2) * 32 + (n // 4) * 16 + n % 2, 8, stride=2), :] = part

    def pick_xz(px, carry):
        found = []
        for n in range(4):
            row_of = inv_xz[pl.ds(pl.multiple_of((n // 2) * 128 + px * 16 + (n % 2) * 8, 8), 8), :]
            found += [jnp.where(bands[k] == px, row_of, carry[n * 4 + k]) for k in range(4)]
        return tuple(found)

    for n, part in enumerate(lax.fori_loop(0, 8, pick_xz, (zero,) * 16)):
        k, n = n % 4, n // 4
        to = (k // 2) * 64 + (n // 2) * 32 + (k % 2) * 16 + (n % 2) * 8
        chosen[to : to + 8, :] = part
    finish(sent)
    finish(share(g.at[pl.ds(pl.multiple_of(y * 64, 64), 64)], on_y, 50))

    own, other = solve(g[...], fwd_y, fwd_xz, spectral, chosen, near_y)
    mine_s[:, 0:96] = other
    sent = start([remote(mine_s, peer_s, 53, mate(1))])
    finish(sent)
    share_s[:, 0:96] = own + peer_s[:, 0:96]
    stores += start([pltpu.make_async_copy(share_s, share_hbm, out_sem.at[2])])
    drain()
    for copy in stores:
        copy.wait()


def halves(table):
    high = table.astype(ml_dtypes.bfloat16).astype(np.float64)
    low = (table - high).astype(ml_dtypes.bfloat16).astype(np.float64)
    return high, low


def solve_tables():
    space = np.arange(128)
    px, ix, iz = space // 16, (space // 4) % 4, space % 4
    x, z = 4 * px + ix, iz
    kx, kz = space // 4, space % 4
    iy, py = space // 32, space % 32
    y = 4 * py + iy
    ky = space
    theta = 2.0 * np.pi * ((kx[:, None] * x[None, :] % 32) / 32.0 + (kz[:, None] * z[None, :] % 4) / 4.0)
    phi = 2.0 * np.pi * ((y[:, None] * ky[None, :]) % 128) / 128.0
    high, low = halves(np.concatenate([np.cos(phi), -np.sin(phi)], axis=1))
    fwd_y = np.concatenate([high, high, low], axis=0)
    high, low = halves(np.concatenate([np.cos(theta), np.sin(theta)], axis=0))
    fwd_xz = np.concatenate([high, low], axis=1)
    inv_xz = np.concatenate([np.cos(theta.T), np.sin(theta.T)], axis=0).astype(np.float32)
    line = np.arange(256)
    turn = 2.0 * np.pi * (((4 * (line // 8) + (line % 8) // 2)[:, None] * ky[None, :]) % 128) / 128.0
    inv_y = (np.concatenate([np.cos(turn), -np.sin(turn)], axis=1) / 16384.0).astype(np.float32)

    def waves(index, length):
        signed = np.where(index < (length + 1) // 2, index, index - length)
        full = signed * (2.0 * math.pi / length)
        return full, np.where(index == length // 2, 0.0, full)

    full_x, slope_x = waves(kx, GX)
    full_y, slope_y = waves(ky, GY)
    full_z, slope_z = waves(kz, GZ)
    square = (full_x**2 + full_z**2)[:, None] + (full_y**2)[None, :]
    inverse = np.where(square > 0, 1.0 / np.where(square > 0, square, 1.0), 0.0)
    spectral = np.concatenate([inverse * slope_x[:, None], inverse * slope_y[None, :], inverse * slope_z[:, None]])
    src = np.arange(96)
    row = np.arange(192)
    src_c, src_b, src_ix, src_iz = src // 32, (src // 16) % 2, (src // 4) % 4, src % 4
    match = ((src_c * 4 + src_ix)[None, :] == (row // 16)[:, None]) & (src_b[None, :] == (row % 2)[:, None])
    spread_z = src_iz[:, None] == ((np.arange(128) % 32) // 8)[None, :]
    return tuple(a.astype(np.float32) for a in (inv_xz, inv_y, fwd_y, fwd_xz, spectral, match * 1.0, spread_z * 1.0))


def cut(array):
    high = array.astype(jnp.bfloat16)
    return high, (array - high.astype(jnp.float32)).astype(jnp.bfloat16)


def thirds(array):
    high = array.astype(jnp.bfloat16)
    rest = array - high.astype(jnp.float32)
    middle = rest.astype(jnp.bfloat16)
    return high, middle, (rest - middle.astype(jnp.float32)).astype(jnp.bfloat16)


def dot(left, right):
    return jnp.dot(left, right, preferred_element_type=jnp.float32)


def dot_nt(left, right):
    return lax.dot_general(left, right, (((1,), (1,)), ((), ())), preferred_element_type=jnp.float32)


def solve(sent, fwd_y, fwd_xz, spectral, chosen, near_y):
    hot = (sent[:, 192:193] == iota((256, 256), 1).astype(jnp.float32)).astype(jnp.bfloat16)
    high, low = cut(sent.T)
    columns = dot(high, hot) + dot(low, hot)
    lane = iota((48, 128), 1)
    rows = []
    for px in range(8):
        held = None
        for iy in range(4):
            part = columns[iy * 48 : iy * 48 + 48, (px // 4) * 128 : (px // 4) * 128 + 128]
            turn = ((iy - px % 4) * 32) % 128
            if turn:
                part = pltpu.roll(part, turn, 1)
            held = part if held is None else jnp.where(lane >= iy * 32, part, held)
        rows.append(held)
    high, low = cut(jnp.concatenate(rows, axis=0))
    table = fwd_y[...].astype(jnp.bfloat16)
    waves_y = dot(jnp.concatenate([high, low], axis=1), table[0:256]) + dot(high, table[256:384])
    stacked = jnp.concatenate(
        [
            jnp.concatenate([waves_y[px * 48 + c * 16 : px * 48 + c * 16 + 16, :] for px in range(8)], axis=0)
            for c in range(3)
        ],
        axis=1,
    )
    high, low = cut(stacked)
    table = fwd_xz[...].astype(jnp.bfloat16)
    full = dot(table, jnp.concatenate([high, high], axis=0)) + dot(table[:, 0:128], low)
    slope_x, slope_y, slope_z = spectral[0:128, :], spectral[128:256, :], spectral[256:384, :]
    real, imag = [], []
    for c in range(3):
        low = full[:, c * 256 : c * 256 + 128]
        high = full[:, c * 256 + 128 : c * 256 + 256]
        real.append(low[0:128] + high[128:256])
        imag.append(high[0:128] - low[128:256])

    def cross(hat):
        return [
            slope_y * hat[2] - slope_z * hat[1],
            slope_z * hat[0] - slope_x * hat[2],
            slope_x * hat[1] - slope_y * hat[0],
        ]

    cross_real, cross_imag = cross(real), cross(imag)
    high, low = cut(jnp.concatenate([part for c in range(3) for part in (-cross_imag[c], cross_real[c])], axis=1))
    chosen_high, chosen_low = cut(chosen[...])
    near = dot(jnp.concatenate([chosen_high, chosen_low], axis=1), jnp.concatenate([high, high], axis=0))
    near = near + dot(chosen_high, low)
    shares = []
    for side in range(2):
        lines = []
        for c in range(3):
            low = near[side * 64 : side * 64 + 64, c * 256 : c * 256 + 128]
            high = near[side * 64 : side * 64 + 64, c * 256 + 128 : c * 256 + 256]
            lines.append(jnp.concatenate([low[0:32] - high[32:64], high[0:32] + low[32:64]], axis=1))
        high, low = cut(jnp.concatenate(lines, axis=0))
        near_high, near_low = cut(jnp.concatenate([near_y[side * 32 + n * 16 : side * 32 + n * 16 + 16, :] for n in range(2)], axis=1))
        shares.append(dot_nt(near_high, high) + (dot_nt(near_high, low) + dot_nt(near_low, high)))
    return shares


def lift(share, match, spread_z):
    high, low = cut(jnp.concatenate([share] * 12, axis=0) * match[...])
    table = spread_z[...].astype(jnp.bfloat16)
    return dot(high, table) + dot(low, table)


def final_kernel(both_hbm, share_hbm, fresh_hbm, match_hbm, spread_hbm, fresh_out, out_hbm,
                 both, share, fresh, match, spread_z, field, moved, sem, out_sem):
    halves_of = [pl.ds(n * 64, 64) for n in range(2)]
    loads = [pltpu.make_async_copy(share_hbm, share, sem.at[0])]
    loads += [pltpu.make_async_copy(both_hbm.at[part], both.at[part], sem.at[1 + n]) for n, part in enumerate(halves_of)]
    loads += [pltpu.make_async_copy(fresh_hbm, fresh, sem.at[3])]
    tables = [pltpu.make_async_copy(match_hbm, match, sem.at[4]), pltpu.make_async_copy(spread_hbm, spread_z, sem.at[5])]
    for load in loads[:1] + tables + loads[1:]:
        load.start()
    for load in loads[:1] + tables:
        load.wait()
    field[...] = lift(share[:, 0:96], match, spread_z)
    stores = []
    for n in range(2):
        loads[1 + n].wait()
        for ix in (n * 2, n * 2 + 1):
            lifted = [[field[(c * 4 + ix) * 16 + h * 8 : (c * 4 + ix) * 16 + h * 8 + 8, :] for h in range(2)] for c in range(3)]
            for x in range(ix * 8, ix * 8 + 8):
                at = n * 64 + x % 16
                for h in range(2):
                    rows = slice(h * 8, h * 8 + 8)
                    scale = both[at + 48, rows, :]
                    for c in range(3):
                        moved[c, x, rows, :] = both[at + c * 16, rows, :] + lifted[c][h] * scale
        planes = pl.ds(n * 16, 16)
        stores.append(pltpu.make_async_copy(moved.at[:, planes], out_hbm.at[:, planes], out_sem.at[n]))
        stores[-1].start()
    loads[3].wait()
    stores.append(pltpu.make_async_copy(fresh, fresh_out, out_sem.at[2]))
    stores[-1].start()
    for copy in stores:
        copy.wait()


SMEM = pl.BlockSpec(memory_space=pltpu.SMEM)
ANY = pl.BlockSpec(memory_space=pl.ANY)
LIMIT = 62 * 2**20


def f32(*shape):
    return jax.ShapeDtypeStruct(shape, jnp.float32)


def scratch(*shape):
    return pltpu.VMEM(shape, jnp.float32)


def split(array):
    return array.reshape(2, 3, 256, 128).transpose(1, 2, 0, 3)


def join(array):
    return array.reshape(3, 256, 2, 128).transpose(2, 0, 1, 3).reshape(2, 3, 32768)


def body(vorticity, velocity, level_map, patch_owner, neighbours, fish_slot, fish_mask, fish_speed):
    w, u = split(vorticity), split(velocity)
    w, u = w.reshape(96, 16, 128), u.reshape(96, 16, 128)
    field = f32(96, 16, 128)

    def faces(count):
        return [scratch(rows * count, 128) for rows in (96, 192, 96, 96)]

    *tables, match, spread_z = (jnp.asarray(a) for a in fold_tables() + solve_tables())
    sources = (w, u, fish_mask.reshape(256, 128), *tables)
    fresh, both, share = pl.pallas_call(
        front_kernel,
        out_shape=(field, f32(128, 16, 128), f32(16, 128)),
        in_specs=[SMEM] * 4 + [ANY] * 12,
        out_specs=(ANY,) * 3,
        scratch_shapes=[
            *(scratch(*array.shape) for array in sources),
            scratch(96, 16, 128),
            scratch(128, 16, 128),
            *faces(4),
            *faces(2),
            scratch(192, 128),
            pltpu.VMEM((8, 128), jnp.int32),
            pltpu.VMEM((64, 128), jnp.int32),
            scratch(192, 128),
            scratch(32, 128),
            scratch(256, 256),
            scratch(128, 128),
            scratch(64, 128),
            scratch(16, 128),
            scratch(16, 128),
            scratch(16, 128),
            pltpu.SMEM((1,), jnp.int32),
            pltpu.SemaphoreType.DMA((12,)),
            pltpu.SemaphoreType.DMA((3,)),
            pltpu.SemaphoreType.DMA((56,)),
            pltpu.SemaphoreType.DMA((56,)),
        ],
        compiler_params=pltpu.CompilerParams(collective_id=0, has_side_effects=True, vmem_limit_bytes=LIMIT),
        name="front",
    )(neighbours, level_map, patch_owner, fish_speed, fish_slot, *sources)
    fresh, moved = pl.pallas_call(
        final_kernel,
        out_shape=(field, f32(3, 32, 16, 128)),
        in_specs=[ANY] * 5,
        out_specs=(ANY, ANY),
        scratch_shapes=[
            scratch(128, 16, 128),
            scratch(16, 128),
            scratch(96, 16, 128),
            scratch(192, 96),
            scratch(96, 128),
            scratch(192, 128),
            scratch(3, 32, 16, 128),
            pltpu.SemaphoreType.DMA((6,)),
            pltpu.SemaphoreType.DMA((3,)),
        ],
        compiler_params=pltpu.CompilerParams(vmem_limit_bytes=LIMIT),
        name="final",
    )(both, share, fresh, match, spread_z)
    return join(fresh), join(moved)


def solution(mesh):
    blocks = ("blk", "sub")
    placed = (
        P(blocks, None, None),
        P(blocks, None, None),
        P(blocks),
        P(blocks),
        P(blocks, None),
        P(blocks),
        P(blocks, None),
        P(blocks, None),
    )
    return jax.shard_map(
        body,
        mesh=mesh,
        in_specs=placed,
        out_specs=(P(blocks, None, None), P(blocks, None, None)),
        check_vma=False,
    )
```
